512 devices in a mesh: ha: 16 (over z_hi, x, core), wa: 32 (over z_lo, y).
Axes of the slice: x: 4, y: 4, z: 16 (z_hi: 2, z_lo: 8; z = z_hi * 8 + z_lo), core: 2. Of those that a mesh axis runs over, the one named last changes fastest.
Arguments:
- queries: bfloat16 [256, 448, 1024], P('ha', 'wa'), may hold values from -6 to 6, as said below
- kv_new: bfloat16 [2, 256, 448, 1024], P(None, 'ha', 'wa'), may hold values from -24 to 24
- kv_past: bfloat16 [2, 2, 256, 448, 1024], P(None, None, 'ha', 'wa'), may hold values from -24 to 24
Outputs:
- attended: bfloat16 [256, 448, 1024], P('ha', 'wa')
The draws below stay inside these ranges and needn't reach their ends.
Inputs may be any that keep to these rules, and one draw needn't show every extreme that they name: `queries`: query entries.
All inputs are finite; a program needn't handle non-finite values.
Results may differ from the reference program's by a relative error of at most 0.0049.
Values may be sent and summed in bfloat16 or wider, within the bound.
A program may use at most 128 MiB of HBM per device.

```python
import math
import jax
import jax.numpy as jnp
from jax import lax

HEADS = 8
HEAD_DIM = 128
RADIUS = 4
PAST = 2
HD = 1024
FH = 256
FW = 448


def drawn_keys(key):
    return jnp.clip(jax.random.normal(key, (FH, FW, HD), jnp.float32), -6.0, 6.0)


def drawn_values(key):
    return jnp.clip(4.0 * jax.random.normal(key, (FH, FW, HD), jnp.float32), -24.0, 24.0)


def draw_queries(key, part):
    key = jax.random.fold_in(key, 1)
    return drawn_keys(key).astype(jnp.bfloat16)


def draw_kv_new(key, part):
    key = jax.random.fold_in(key, 2)
    key_part, value_part = jax.random.split(key)
    keys_drawn = drawn_keys(key_part)
    values_drawn = drawn_values(value_part)
    return jnp.stack([keys_drawn, values_drawn], 0).astype(jnp.bfloat16)


def draw_kv_past(key, part):
    key = jax.random.fold_in(key, 3)
    frames_out = []
    for frame_index in range(PAST):
        key_part, value_part = jax.random.split(jax.random.fold_in(key, frame_index))
        keys_drawn = drawn_keys(key_part)
        values_drawn = drawn_values(value_part)
        frames_out.append(jnp.stack([keys_drawn, values_drawn], 0))
    return jnp.stack(frames_out, 0).astype(jnp.bfloat16)


def setup_inputs(seed: int = 0) -> dict:
    key_of = jax.random.split(jax.random.key(seed), 4)
    return {
        "queries": draw_queries(jax.random.fold_in(key_of[3], 71), 0),
        "kv_new": draw_kv_new(jax.random.fold_in(key_of[3], 71), 0),
        "kv_past": draw_kv_past(jax.random.fold_in(key_of[3], 71), 0),
    }


def reference(queries, kv_new, kv_past):
    score_scale = 1.0 / math.sqrt(HEAD_DIM)
    side_cells = 2 * RADIUS + 1
    key_frames = jnp.concatenate([kv_past[:, 0], kv_new[0][None]], 0)
    value_frames = jnp.concatenate([kv_past[:, 1], kv_new[1][None]], 0)
    pad_spec = ((0, 0), (RADIUS, RADIUS), (RADIUS, RADIUS), (0, 0))
    key_padded = jnp.pad(key_frames, pad_spec)
    value_padded = jnp.pad(value_frames, pad_spec)
    inside = jnp.pad(jnp.ones((FH, FW), jnp.float32), RADIUS)
    offsets = jnp.arange((PAST + 1) * side_cells * side_cells, dtype=jnp.int32)
    query_wide = queries.astype(jnp.float32).reshape(FH, FW, HEADS, HEAD_DIM)
    anchor = jnp.zeros((), jnp.int32)

    def split_offset(offset):
        frame_index = (offset // (side_cells * side_cells)).astype(jnp.int32)
        row_shift = (offset // side_cells % side_cells).astype(jnp.int32)
        col_shift = (offset % side_cells).astype(jnp.int32)
        return (frame_index, row_shift, col_shift)

    def score_at(offset):
        frame_index, row_shift, col_shift = split_offset(offset)
        key_slice = lax.dynamic_slice(key_padded, (frame_index, row_shift, col_shift, anchor), (1, FH, FW, HD))[0]
        key_wide = key_slice.astype(jnp.float32).reshape(FH, FW, HEADS, HEAD_DIM)
        scores = lax.optimization_barrier(jnp.sum(query_wide * key_wide, -1)) * score_scale
        allowed = lax.dynamic_slice(inside, (row_shift, col_shift), (FH, FW))
        return jnp.where(allowed[:, :, None] > 0.5, scores, -1e+30)
    scores = lax.map(score_at, offsets)
    row_max = lax.optimization_barrier(jnp.max(scores, 0))
    weights_raw = jnp.exp(scores - row_max[None])
    probs = (weights_raw / lax.optimization_barrier(jnp.sum(weights_raw, 0))[None]).astype(jnp.bfloat16)

    def accumulate(total, offset_prob):
        offset, prob = offset_prob
        frame_index, row_shift, col_shift = split_offset(offset)
        value_slice = lax.dynamic_slice(value_padded, (frame_index, row_shift, col_shift, anchor), (1, FH, FW, HD))[0]
        value_wide = value_slice.astype(jnp.float32).reshape(FH, FW, HEADS, HEAD_DIM)
        return (total + prob.astype(jnp.float32)[..., None] * value_wide, None)
    start_total = jnp.zeros((FH, FW, HEADS, HEAD_DIM), jnp.float32)
    total, unused = lax.scan(accumulate, start_total, (offsets, probs))
    return total.reshape(FH, FW, HD).astype(jnp.bfloat16)
```

```python
import functools
import math

import jax
import jax.numpy as jnp
from jax import lax
from jax.experimental import pallas as pl
from jax.experimental.pallas import tpu as pltpu
from jax.sharding import PartitionSpec as P

MESH = pl.DeviceIdType.MESH
HEADS = 8
DIM = 128
RADIUS = 4
FRAMES = 3
ROWS = 16
COLS = 14
PAD = 16
TOKENS = ROWS * PAD
SIDE = ROWS * RADIUS
EDGE = RADIUS * PAD
CORNER = RADIUS * RADIUS
CHUNKS = 4
LOW = -1e30
FOLD = math.log2(math.e) / math.sqrt(DIM)
F32 = jnp.float32
BF16 = jnp.bfloat16


def dot_nt(a, b):
    return lax.dot_general(a, b, (((1,), (1,)), ((), ())), preferred_element_type=F32)


def dot_nn(a, b, precision=None):
    return lax.dot_general(
        a, b, (((1,), (0,)), ((), ())), preferred_element_type=F32, precision=precision
    )


def iota(shape, dim):
    return lax.broadcasted_iota(jnp.int32, shape, dim)


def lanes(head):
    return pl.ds(pl.multiple_of(head * DIM, DIM), DIM)


def kernel(
    nh, nw,
    q_hbm, new_hbm, past_hbm, out_hbm,
    q_in, kv_in, out_v, q_all, kv_all, q_side, kv_side,
    q_edge, q_flank, ext, own_o, own_m, own_l,
    send_o, send_s, edge_o, edge_s, flank_o, flank_s,
    bias_own, bias_flank, bias_edge, pick, side_stat,
    load_sem, store_sem,
    q_edge_sem, q_flank_sem, ext_sem, edge_sem, flank_sem, stat_sem,
):
    h = lax.axis_index("ha")
    w = lax.axis_index("wa")
    has_up, has_down = h > 0, h < nh - 1
    has_left, has_right = w > 0, w < nw - 1
    up, down = (h - 1, w), (h + 1, w)
    left, right = (h, w - 1), (h, w + 1)
    flip = (h == nh // 2).astype(jnp.int32)

    barrier = pltpu.get_barrier_semaphore()
    for there, device in ((has_up, up), (has_down, down), (has_left, left), (has_right, right)):
        @pl.when(there)
        def _():
            pl.semaphore_signal(barrier, inc=1, device_id=device, device_id_type=MESH)

    loads = [pltpu.make_async_copy(q_hbm, q_in, load_sem.at[0])]
    for kv in range(2):
        for f in range(FRAMES):
            source = new_hbm.at[kv] if f == FRAMES - 1 else past_hbm.at[f, kv]
            slot = kv * FRAMES + f
            loads.append(pltpu.make_async_copy(source, kv_in.at[slot], load_sem.at[1 + slot]))
    for load in loads:
        load.start()

    qi, ki = iota((TOKENS, TOKENS), 0), iota((TOKENS, TOKENS), 1)
    near = (
        (abs(qi // PAD - ki // PAD) <= RADIUS)
        & (abs(qi % PAD - ki % PAD) <= RADIUS)
        & (ki % PAD < COLS)
    )
    bias_own[...] = jnp.where(near, 0.0, LOW)

    qi, ki = iota((SIDE, FRAMES * SIDE), 0), iota((SIDE, FRAMES * SIDE), 1) % SIDE
    rows_near = abs(qi // RADIUS - ki // RADIUS) <= RADIUS
    bias_flank[0] = jnp.where(rows_near & (ki % RADIUS <= qi % RADIUS), 0.0, LOW)
    bias_flank[1] = jnp.where(rows_near & (ki % RADIUS >= qi % RADIUS), 0.0, LOW)

    span = EDGE + 2 * CORNER
    qi, ki = iota((EDGE, FRAMES * span), 0), iota((EDGE, FRAMES * span), 1) % span
    in_left = (ki >= EDGE) & (ki < EDGE + CORNER)
    in_right = ki >= EDGE + CORNER
    corner = (ki - EDGE) % CORNER
    key_row = jnp.where(ki < EDGE, ki // PAD, corner // RADIUS)
    key_col = jnp.where(
        ki < EDGE,
        ki % PAD,
        jnp.where(in_left, corner % RADIUS - RADIUS, corner % RADIUS + COLS),
    )
    real = jnp.where(
        in_left,
        has_left.astype(jnp.int32),
        jnp.where(in_right, has_right.astype(jnp.int32), (ki % PAD < COLS).astype(jnp.int32)),
    )
    cols_near = (abs(qi % PAD - key_col) <= RADIUS) & (real > 0)
    bias_edge[0] = jnp.where(cols_near & (key_row <= qi // PAD), 0.0, LOW)
    bias_edge[1] = jnp.where(cols_near & (key_row >= qi // PAD), 0.0, LOW)

    pi, pt = iota((2 * SIDE, TOKENS), 0), iota((2 * SIDE, TOKENS), 1)
    pl_token = pi % SIDE // RADIUS * PAD + pi % RADIUS + jnp.where(pi < SIDE, 0, COLS - RADIUS)
    pick[...] = jnp.where(pt == pl_token, 1.0, 0.0).astype(BF16)

    q_all[...] = jnp.zeros_like(q_all)
    for slot in range(2 * FRAMES):
        kv_all[slot] = jnp.zeros_like(kv_all[slot])

    loads[0].wait()
    for r in range(ROWS):
        q_all[r * PAD : r * PAD + COLS, :] = q_in[r]
    q_side[...] = dot_nn(pick[...], q_all[...]).astype(BF16)

    for there, side in ((has_up, 0), (has_down, 1)):
        @pl.when(jnp.logical_not(there))
        def _():
            edge_o[side] = jnp.zeros_like(edge_o[side])
            edge_s[side] = jnp.full(edge_s.shape[1:], LOW, F32)
    for there, side in ((has_left, 0), (has_right, 1)):
        @pl.when(jnp.logical_not(there))
        def _():
            flank_o[side * SIDE : (side + 1) * SIDE, :] = jnp.zeros((SIDE, HEADS * DIM), BF16)
            flank_s[side] = jnp.full(flank_s.shape[1:], LOW, F32)
            for s in range(2):
                ext[s, :, side * CORNER : (side + 1) * CORNER, :] = jnp.zeros(
                    (2 * FRAMES, CORNER, HEADS * DIM), BF16
                )

    def remote(src, dst, sems, index, device):
        return pltpu.make_async_remote_copy(
            src_ref=src,
            dst_ref=dst,
            send_sem=sems.at[(0, *index)],
            recv_sem=sems.at[(1, *index)],
            device_id=device,
            device_id_type=MESH,
        )

    width = HEADS * DIM // CHUNKS

    def copy_q_edge(side, c, device):
        part = pl.ds(c * width, width)
        first = (1 - side) * (TOKENS - EDGE)
        return remote(
            q_all.at[pl.ds(first, EDGE), part],
            q_edge.at[side, :, part],
            q_edge_sem,
            (side, c),
            device,
        )

    def copy_q_flank(side, device):
        return remote(
            q_side.at[pl.ds((1 - side) * SIDE, SIDE)],
            q_flank.at[side],
            q_flank_sem,
            (side,),
            device,
        )

    def copy_ext(side, s, device):
        return remote(
            kv_side.at[:, pl.ds((1 - side) * SIDE + s * (SIDE - CORNER), CORNER)],
            ext.at[s, :, pl.ds(side * CORNER, CORNER)],
            ext_sem,
            (side, s),
            device,
        )

    def copy_edge_o(side, c, device):
        part = pl.ds(c * width, width)
        return remote(
            send_o.at[side, :, part],
            edge_o.at[1 - side, :, part],
            edge_sem,
            (1 - side, c),
            device,
        )

    def copy_edge_s(side, device):
        return remote(send_s.at[side], edge_s.at[1 - side], stat_sem, (1 - side,), device)

    def copy_flank_o(side, device):
        return remote(
            send_o.at[2 + side],
            flank_o.at[pl.ds((1 - side) * SIDE, SIDE)],
            flank_sem,
            (1 - side,),
            device,
        )

    def copy_flank_s(side, device):
        return remote(send_s.at[2 + side], flank_s.at[1 - side], stat_sem, (3 - side,), device)

    n_near = (
        has_up.astype(jnp.int32)
        + has_down.astype(jnp.int32)
        + has_left.astype(jnp.int32)
        + has_right.astype(jnp.int32)
    )
    pl.semaphore_wait(barrier, n_near)

    for c in range(CHUNKS):
        @pl.when(has_down)
        def _():
            copy_q_edge(0, c, down).start()

        @pl.when(has_up)
        def _():
            copy_q_edge(1, c, up).start()

    @pl.when(has_right)
    def _():
        copy_q_flank(0, right).start()

    @pl.when(has_left)
    def _():
        copy_q_flank(1, left).start()

    for slot in range(2 * FRAMES):
        loads[1 + slot].wait()
        for r in range(ROWS):
            kv_all[slot, r * PAD : r * PAD + COLS, :] = kv_in[slot, r]
        kv_side[slot] = dot_nn(pick[...], kv_all[slot]).astype(BF16)

    for s in range(2):
        @pl.when(has_right)
        def _():
            copy_ext(0, s, right).start()

        @pl.when(has_left)
        def _():
            copy_ext(1, s, left).start()

    def soft(scores, top):
        return jnp.exp2(scores * FOLD - top).astype(BF16)

    def with_ones(values):
        return jnp.concatenate([values, jnp.ones_like(values)], axis=1)

    half = TOKENS // 2
    cut = TOKENS - EDGE

    def own_head(head, carry):
        at = lanes(head)
        q = q_all[:, at]
        k0, k1 = [
            jnp.concatenate([kv_all[f, pl.ds(b * half, half), at] for f in range(FRAMES)], axis=0)
            for b in range(2)
        ]
        v0, v1 = [
            jnp.concatenate(
                [kv_all[FRAMES + f, pl.ds(b * half, half), at] for f in range(FRAMES)], axis=0
            )
            for b in range(2)
        ]
        b0 = bias_own[0:cut, 0:half]
        b1 = bias_own[EDGE:TOKENS, half:TOKENS]
        s0 = dot_nt(q[0:cut], k0) + jnp.concatenate([b0] * FRAMES, axis=1)
        s1 = dot_nt(q[EDGE:TOKENS], k1) + jnp.concatenate([b1] * FRAMES, axis=1)
        t0 = jnp.max(s0, axis=1, keepdims=True)
        t1 = jnp.max(s1, axis=1, keepdims=True)
        top = FOLD * jnp.concatenate(
            [t0[0:EDGE], jnp.maximum(t0[EDGE:cut], t1[0 : cut - EDGE]), t1[cut - EDGE :]], axis=0
        )
        o0 = dot_nn(soft(s0, top[0:cut]), with_ones(v0))
        o1 = dot_nn(soft(s1, top[EDGE:TOKENS]), with_ones(v1))
        both = jnp.concatenate(
            [o0[0:EDGE], o0[EDGE:cut] + o1[0 : cut - EDGE], o1[cut - EDGE :]], axis=0
        )
        own_o[head] = both[:, :DIM]
        own_l[head] = both[:, DIM:]
        own_m[head] = jnp.broadcast_to(top, (TOKENS, DIM))
        return carry

    lax.fori_loop(0, HEADS, own_head, 0)

    lane = iota((PAD, DIM), 1)

    def guest_head(head, stat, q, k, v, bias):
        s = dot_nt(q, k) + bias
        top = FOLD * jnp.max(s, axis=1, keepdims=True)
        both = dot_nn(soft(s, top), with_ones(v))
        for t in range(RADIUS):
            group = slice(t * PAD, (t + 1) * PAD)
            stat = jnp.where(lane == 32 * t + head, top[group], stat)
            stat = jnp.where(lane == 32 * t + HEADS + head, both[group, DIM:], stat)
        return both[:, :DIM].astype(BF16), stat

    for side, there, device in ((0, has_left, left), (1, has_right, right)):
        @pl.when(there)
        def _():
            copy_q_flank(side, device).wait_recv()

            def flank_head(head, stat):
                at = lanes(head)
                part = pl.ds(side * SIDE, SIDE)
                k = jnp.concatenate([kv_side[f, part, at] for f in range(FRAMES)], axis=0)
                v = jnp.concatenate([kv_side[FRAMES + f, part, at] for f in range(FRAMES)], axis=0)
                o, stat = guest_head(head, stat, q_flank[side, :, at], k, v, bias_flank[side])
                send_o[2 + side, :, at] = o
                return stat

            send_s[2 + side] = lax.fori_loop(0, HEADS, flank_head, jnp.zeros((PAD, DIM), F32))
            copy_flank_o(side, device).start()
            copy_flank_s(side, device).start()

    for side, there, device in ((0, has_left, left), (1, has_right, right)):
        @pl.when(there)
        def _():
            for s in range(2):
                copy_ext(side, s, device).wait_recv()

    per = HEADS // CHUNKS
    for turn in range(2):
        side = (turn + flip) % 2
        there = jnp.where(side == 0, has_up.astype(jnp.int32), has_down.astype(jnp.int32)) > 0
        device = (h - 1 + 2 * side, w)

        @pl.when(there)
        def _():
            def edge_chunk(c, stat):
                copy_q_edge(side, c, device).wait_recv()

                def edge_head(i, stat):
                    head = c * per + i
                    at = lanes(head)
                    part = pl.ds(pl.multiple_of(side * (TOKENS - EDGE), EDGE), EDGE)

                    def keys(kv):
                        pieces = []
                        for f in range(FRAMES):
                            pieces.append(kv_all[kv * FRAMES + f, part, at])
                            pieces.append(ext[side, kv * FRAMES + f, :, at])
                        return jnp.concatenate(pieces, axis=0)

                    o, stat = guest_head(
                        head, stat, q_edge[side, :, at], keys(0), keys(1), bias_edge[side]
                    )
                    send_o[side, :, at] = o
                    return stat

                for i in range(per):
                    stat = edge_head(i, stat)
                copy_edge_o(side, c, device).start()
                return stat

            stat = jnp.zeros((PAD, DIM), F32)
            for c in range(CHUNKS):
                stat = edge_chunk(c, stat)
            send_s[side] = stat
            copy_edge_s(side, device).start()

    for side, there, device in ((0, has_left, left), (1, has_right, right)):
        @pl.when(there)
        def _():
            copy_flank_o(1 - side, device).wait_recv()
            copy_flank_s(1 - side, device).wait_recv()

    packed = []
    for side in range(2):
        for t in range(RADIUS):
            packed.append(pltpu.roll(flank_s[side], (DIM - 32 * t) % DIM, 1) if t else flank_s[side])
    side_stat[...] = lax.dot_general(
        pick[...].astype(F32),
        jnp.concatenate(packed, axis=0),
        (((0,), (0,)), ((), ())),
        preferred_element_type=F32,
        precision=lax.Precision.HIGHEST,
    )
    spot = iota((TOKENS, DIM), 0) % PAD
    covered = (spot < RADIUS) | ((spot >= COLS - RADIUS) & (spot < COLS))
    wide_lane = iota((TOKENS, DIM), 1)

    def column(stat, where, index, fill):
        return jnp.max(jnp.where(where == index, stat, fill), axis=1, keepdims=True)

    def merge_flank(head, carry):
        at = lanes(head)
        stat = side_stat[...]
        m1 = jnp.where(covered, column(stat, wide_lane, head, LOW), LOW)
        l1 = jnp.where(covered, jnp.maximum(column(stat, wide_lane, head + HEADS, LOW), 0.0), 0.0)
        o1 = lax.dot_general(
            pick[...], flank_o[:, at], (((0,), (0,)), ((), ())), preferred_element_type=F32
        )
        m0 = own_m[head]
        top = jnp.maximum(m0, m1)
        a0, a1 = jnp.exp2(m0 - top), jnp.exp2(m1 - top)
        total = a0 * own_l[head] + a1 * l1
        mixed = a0 * own_o[head] + a1 * o1
        own_m[head] = top
        own_l[head] = total
        own_o[head] = mixed
        done = (mixed / total).astype(BF16)
        for r in range(RADIUS, ROWS - RADIUS):
            out_v[r, :, at] = done[r * PAD : r * PAD + COLS]
        return carry

    lax.fori_loop(0, HEADS, merge_flank, 0)
    middle = pl.ds(RADIUS, ROWS - 2 * RADIUS)
    store_middle = pltpu.make_async_copy(out_v.at[middle], out_hbm.at[middle], store_sem.at[0])
    store_middle.start()

    stores = []
    for turn in range(2):
        side = (turn + flip) % 2
        there = jnp.where(side == 0, has_up.astype(jnp.int32), has_down.astype(jnp.int32)) > 0
        device = (h - 1 + 2 * side, w)

        @pl.when(there)
        def _():
            for c in range(CHUNKS):
                copy_edge_o(1 - side, c, device).wait_recv()
            copy_edge_s(1 - side, device).wait_recv()

        part = pl.ds(pl.multiple_of(side * (TOKENS - EDGE), EDGE), EDGE)
        first = side * (ROWS - RADIUS)

        def merge_edge(head, carry):
            at = lanes(head)
            stat = edge_s[side]
            m1 = jnp.concatenate([column(stat, lane, 32 * t + head, LOW) for t in range(RADIUS)], axis=0)
            l1 = jnp.concatenate(
                [column(stat, lane, 32 * t + HEADS + head, LOW) for t in range(RADIUS)], axis=0
            )
            l1 = jnp.maximum(l1, 0.0)
            m0 = own_m[head, part]
            top = jnp.maximum(m0, m1)
            a0, a1 = jnp.exp2(m0 - top), jnp.exp2(m1 - top)
            total = a0 * own_l[head, part] + a1 * l1
            mixed = a0 * own_o[head, part] + a1 * edge_o[side, :, at].astype(F32)
            done = (mixed / total).astype(BF16)
            for t in range(RADIUS):
                out_v[first + t, :, at] = done[t * PAD : t * PAD + COLS]
            return carry

        lax.fori_loop(0, HEADS, merge_edge, 0)
        rows = pl.ds(first, RADIUS)
        store = pltpu.make_async_copy(out_v.at[rows], out_hbm.at[rows], store_sem.at[1 + turn])
        store.start()
        stores.append(store)

    for c in range(CHUNKS):
        @pl.when(has_down)
        def _():
            copy_q_edge(0, c, down).wait_send()
            copy_edge_o(1, c, down).wait_send()

        @pl.when(has_up)
        def _():
            copy_q_edge(1, c, up).wait_send()
            copy_edge_o(0, c, up).wait_send()

    @pl.when(has_down)
    def _():
        copy_edge_s(1, down).wait_send()

    @pl.when(has_up)
    def _():
        copy_edge_s(0, up).wait_send()

    for side, there, device in ((0, has_right, right), (1, has_left, left)):
        @pl.when(there)
        def _():
            copy_q_flank(side, device).wait_send()
            for s in range(2):
                copy_ext(side, s, device).wait_send()
            copy_flank_o(1 - side, device).wait_send()
            copy_flank_s(1 - side, device).wait_send()

    store_middle.wait()
    for store in stores:
        store.wait()


def on_device(nh, nw, queries, kv_new, kv_past):
    wide = HEADS * DIM
    span = EDGE + 2 * CORNER
    any_space = pl.BlockSpec(memory_space=pl.ANY)
    dma = pltpu.SemaphoreType.DMA
    return pl.pallas_call(
        functools.partial(kernel, nh, nw),
        out_shape=jax.ShapeDtypeStruct((ROWS, COLS, wide), BF16),
        in_specs=[any_space] * 3,
        out_specs=any_space,
        scratch_shapes=[
            pltpu.VMEM((ROWS, COLS, wide), BF16),
            pltpu.VMEM((2 * FRAMES, ROWS, COLS, wide), BF16),
            pltpu.VMEM((ROWS, COLS, wide), BF16),
            pltpu.VMEM((TOKENS, wide), BF16),
            pltpu.VMEM((2 * FRAMES, TOKENS, wide), BF16),
            pltpu.VMEM((2 * SIDE, wide), BF16),
            pltpu.VMEM((2 * FRAMES, 2 * SIDE, wide), BF16),
            pltpu.VMEM((2, EDGE, wide), BF16),
            pltpu.VMEM((2, SIDE, wide), BF16),
            pltpu.VMEM((2, 2 * FRAMES, 2 * CORNER, wide), BF16),
            pltpu.VMEM((HEADS, TOKENS, DIM), F32),
            pltpu.VMEM((HEADS, TOKENS, DIM), F32),
            pltpu.VMEM((HEADS, TOKENS, DIM), F32),
            pltpu.VMEM((4, SIDE, wide), BF16),
            pltpu.VMEM((4, PAD, DIM), F32),
            pltpu.VMEM((2, EDGE, wide), BF16),
            pltpu.VMEM((2, PAD, DIM), F32),
            pltpu.VMEM((2 * SIDE, wide), BF16),
            pltpu.VMEM((2, PAD, DIM), F32),
            pltpu.VMEM((TOKENS, TOKENS), F32),
            pltpu.VMEM((2, SIDE, FRAMES * SIDE), F32),
            pltpu.VMEM((2, EDGE, FRAMES * span), F32),
            pltpu.VMEM((2 * SIDE, TOKENS), BF16),
            pltpu.VMEM((TOKENS, DIM), F32),
            dma((1 + 2 * FRAMES,)),
            dma((3,)),
            dma((2, 2, CHUNKS)),
            dma((2, 2)),
            dma((2, 2, 2)),
            dma((2, 2, CHUNKS)),
            dma((2, 2)),
            dma((2, 4)),
        ],
        compiler_params=pltpu.CompilerParams(
            collective_id=0, has_side_effects=True, vmem_limit_bytes=48 * 1024 * 1024
        ),
    )(queries, kv_new, kv_past)


def solution(mesh):
    return jax.shard_map(
        functools.partial(on_device, mesh.shape["ha"], mesh.shape["wa"]),
        mesh=mesh,
        in_specs=(P("ha", "wa", None), P(None, "ha", "wa", None), P(None, None, "ha", "wa", None)),
        out_specs=P("ha", "wa", None),
        check_vma=False,
    )
```

```python
import functools
import math

import jax
import jax.numpy as jnp
from jax import lax
from jax.experimental import pallas as pl
from jax.experimental.pallas import tpu as pltpu
from jax.sharding import PartitionSpec as P

MESH = pl.DeviceIdType.MESH
HEADS = 8
DIM = 128
RADIUS = 4
FRAMES = 3
ROWS = 16
COLS = 14
TOKENS = ROWS * COLS
FLANK = RADIUS * ROWS
SLOTS = 16
EDGE = SLOTS * RADIUS
CORNER = RADIUS * RADIUS
SPAN = EDGE + 2 * CORNER
GROUP = 16
CHUNKS = 4
LOW = -1e30
FOLD = math.log2(math.e) / math.sqrt(DIM)
F32 = jnp.float32
BF16 = jnp.bfloat16
CUT = 8 * ROWS
BLOCK1 = TOKENS - CUT
REACH0 = 12 * ROWS
REACH1 = 4 * ROWS
OWN_UNROLL = 8


def dot_nt(a, b):
    return lax.dot_general(a, b, (((1,), (1,)), ((), ())), preferred_element_type=F32)


def dot_nn(a, b):
    return lax.dot_general(a, b, (((1,), (0,)), ((), ())), preferred_element_type=F32)


def iota(shape, dim):
    return lax.broadcasted_iota(jnp.int32, shape, dim)


def lanes(head):
    if isinstance(head, int):
        return pl.ds(head * DIM, DIM)
    return pl.ds(pl.multiple_of(head * DIM, DIM), DIM)


def mask(allowed):
    return jnp.where(allowed, 0.0, LOW)


def edge_col(slot):
    return jnp.where(slot < COLS - RADIUS, slot, slot - (SLOTS - COLS))


def soft(scores, top):
    return jnp.exp2(scores * FOLD - top).astype(BF16)


def with_ones(values):
    return jnp.concatenate([values, jnp.ones_like(values)], axis=1)


def offset(scores):
    top = FOLD * jnp.max(scores, axis=1, keepdims=True)
    return top.astype(BF16).astype(F32)


def kernel(
    nh, nw,
    q_hbm, new_hbm, past_hbm, out,
    q_all, kv_all, q_pack, kv_pack,
    q_edge, q_flank, ext, own_o, own_m, own_l, edge_own_o, edge_own_m, edge_own_l,
    send_o, send_s, edge_o, edge_s, flank_o, flank_s,
    bias0, bias1, bias_flank, bias_edge, pick, spread,
    load_sem, q_edge_sem, q_flank_sem, ext_sem, edge_sem, flank_sem, stat_sem,
):
    h = lax.axis_index("ha")
    w = lax.axis_index("wa")
    has_up, has_down = h > 0, h < nh - 1
    has_left, has_right = w > 0, w < nw - 1
    up, down = (h - 1, w), (h + 1, w)
    left, right = (h, w - 1), (h, w + 1)
    flip = (h == nh // 2).astype(jnp.int32)

    barrier = pltpu.get_barrier_semaphore()
    for there, device in ((has_up, up), (has_down, down), (has_left, left), (has_right, right)):
        @pl.when(there)
        def _():
            pl.semaphore_signal(barrier, inc=1, device_id=device, device_id_type=MESH)

    loads = [pltpu.make_async_copy(q_hbm, q_all, load_sem.at[0])]
    for kv in range(2):
        for f in range(FRAMES):
            source = new_hbm.at[kv] if f == FRAMES - 1 else past_hbm.at[f, kv]
            slot = kv * FRAMES + f
            loads.append(pltpu.make_async_copy(source, kv_all.at[slot], load_sem.at[1 + slot]))
    for load in loads:
        load.start()

    def picked(shape, dim):
        i, t = iota(shape, dim), iota(shape, 1 - dim)
        slot = i % EDGE // RADIUS
        real = (slot < COLS - RADIUS) | (slot >= SLOTS - RADIUS)
        token = edge_col(slot) * ROWS + i % RADIUS + i // EDGE * (ROWS - RADIUS)
        return jnp.where(real & (t == token), 1.0, 0.0).astype(BF16)

    pick[...] = picked((2 * EDGE, TOKENS), 0)
    spread[...] = picked((TOKENS, 2 * EDGE), 1)

    for there, side in ((has_up, 0), (has_down, 1)):
        @pl.when(jnp.logical_not(there))
        def _():
            q_edge[side] = jnp.zeros(q_edge.shape[1:], BF16)
            edge_o[side] = jnp.zeros(edge_o.shape[1:], BF16)
            edge_s[side] = jnp.full(edge_s.shape[1:], LOW, F32)
    for there, side in ((has_left, 0), (has_right, 1)):
        @pl.when(jnp.logical_not(there))
        def _():
            q_flank[side] = jnp.zeros(q_flank.shape[1:], BF16)
            flank_o[side] = jnp.zeros(flank_o.shape[1:], BF16)
            flank_s[side] = jnp.full(flank_s.shape[1:], LOW, F32)
            for s in range(2):
                ext[s, :, side * CORNER : (side + 1) * CORNER, :] = jnp.zeros(
                    (2 * FRAMES, CORNER, HEADS * DIM), BF16
                )

    loads[0].wait()
    q_pack[...] = dot_nn(pick[...], q_all[...]).astype(BF16)

    def remote(src, dst, sems, index, device):
        return pltpu.make_async_remote_copy(
            src_ref=src,
            dst_ref=dst,
            send_sem=sems.at[(0, *index)],
            recv_sem=sems.at[(1, *index)],
            device_id=device,
            device_id_type=MESH,
        )

    width = HEADS * DIM // CHUNKS

    def copy_q_edge(side, c, device):
        part = pl.ds(c * width, width)
        return remote(
            q_pack.at[pl.ds((1 - side) * EDGE, EDGE), part],
            q_edge.at[side, :, part],
            q_edge_sem,
            (side, c),
            device,
        )

    def copy_q_flank(side, device):
        return remote(
            q_all.at[pl.ds((1 - side) * (TOKENS - FLANK), FLANK)],
            q_flank.at[side],
            q_flank_sem,
            (side,),
            device,
        )

    def copy_ext(side, s, device):
        return remote(
            kv_pack.at[:, pl.ds((1 - side) * (EDGE - CORNER) + s * EDGE, CORNER)],
            ext.at[s, :, pl.ds(side * CORNER, CORNER)],
            ext_sem,
            (side, s),
            device,
        )

    def copy_edge_o(side, c, device):
        part = pl.ds(c * width, width)
        return remote(
            send_o.at[side, :, part],
            edge_o.at[1 - side, :, part],
            edge_sem,
            (1 - side, c),
            device,
        )

    def copy_edge_s(side, device):
        return remote(send_s.at[side], edge_s.at[1 - side], stat_sem, (1 - side,), device)

    def copy_flank_o(side, device):
        return remote(send_o.at[2 + side], flank_o.at[1 - side], flank_sem, (1 - side,), device)

    def copy_flank_s(side, device):
        return remote(send_s.at[2 + side], flank_s.at[1 - side], stat_sem, (3 - side,), device)

    n_near = (
        has_up.astype(jnp.int32)
        + has_down.astype(jnp.int32)
        + has_left.astype(jnp.int32)
        + has_right.astype(jnp.int32)
    )
    pl.semaphore_wait(barrier, n_near)

    for c in range(CHUNKS):
        @pl.when(has_down)
        def _():
            copy_q_edge(0, c, down).start()

        @pl.when(has_up)
        def _():
            copy_q_edge(1, c, up).start()

    @pl.when(has_right)
    def _():
        copy_q_flank(0, right).start()

    @pl.when(has_left)
    def _():
        copy_q_flank(1, left).start()

    for slot in range(2 * FRAMES):
        loads[1 + slot].wait()
        kv_pack[slot] = dot_nn(pick[...], kv_all[slot]).astype(BF16)

    for s in range(2):
        @pl.when(has_right)
        def _():
            copy_ext(0, s, right).start()

        @pl.when(has_left)
        def _():
            copy_ext(1, s, left).start()

    q, k = iota(bias0.shape, 0), iota(bias0.shape, 1)
    bias0[...] = mask((abs(q // ROWS - k // ROWS) <= RADIUS) & (abs(q % ROWS - k % ROWS) <= RADIUS))
    q, k = iota(bias1.shape, 0) + REACH1, iota(bias1.shape, 1) + BLOCK1
    bias1[...] = mask(
        (abs(q // ROWS - k // ROWS) <= RADIUS) & (abs(q % ROWS - k % ROWS) <= RADIUS) & (k >= CUT)
    )

    q, k = iota(bias_flank.shape[1:], 0), iota(bias_flank.shape[1:], 1)
    rows_near = (abs(q % ROWS - k % ROWS) <= RADIUS) & (k < FRAMES * FLANK)
    k = k % FLANK
    bias_flank[0] = mask(rows_near & (k // ROWS <= q // ROWS))
    bias_flank[1] = mask(rows_near & (k // ROWS >= q // ROWS))

    q, k = iota((EDGE, FRAMES * SPAN), 0), iota((EDGE, FRAMES * SPAN), 1) % SPAN
    slot = k // RADIUS
    in_left = (k >= EDGE) & (k < EDGE + CORNER)
    in_right = k >= EDGE + CORNER
    key_col = jnp.where(
        in_left, slot - SLOTS - RADIUS, jnp.where(in_right, slot - SLOTS - RADIUS + COLS, edge_col(slot))
    )
    real = jnp.where(
        in_left,
        has_left.astype(jnp.int32),
        jnp.where(
            in_right,
            has_right.astype(jnp.int32),
            ((slot < COLS - RADIUS) | (slot >= SLOTS - RADIUS)).astype(jnp.int32),
        ),
    )
    cols_near = (abs(edge_col(q // RADIUS) - key_col) <= RADIUS) & (real > 0)
    bias_edge[0] = mask(cols_near & (k % RADIUS <= q % RADIUS))
    bias_edge[1] = mask(cols_near & (k % RADIUS >= q % RADIUS))

    def own_head(head):
        at = lanes(head)

        def block(kv, first, size):
            return jnp.concatenate(
                [kv_all[kv * FRAMES + f, pl.ds(first, size), at] for f in range(FRAMES)], axis=0
            )

        s0 = dot_nt(q_all[0:REACH0, at], block(0, 0, CUT)) + jnp.concatenate(
            [bias0[...]] * FRAMES, axis=1
        )
        s1 = dot_nt(q_all[REACH1:TOKENS, at], block(0, BLOCK1, CUT)) + jnp.concatenate(
            [bias1[...]] * FRAMES, axis=1
        )
        t0 = jnp.max(s0, axis=1, keepdims=True)
        t1 = jnp.max(s1, axis=1, keepdims=True)
        both = REACH0 - REACH1
        top = FOLD * jnp.concatenate(
            [t0[0:REACH1], jnp.maximum(t0[REACH1:], t1[0:both]), t1[both:]], axis=0
        )
        top = top.astype(BF16).astype(F32)
        o0 = dot_nn(soft(s0, top[0:REACH0]), with_ones(block(1, 0, CUT)))
        o1 = dot_nn(soft(s1, top[REACH1:TOKENS]), with_ones(block(1, BLOCK1, CUT)))
        o = jnp.concatenate([o0[0:REACH1], o0[REACH1:] + o1[0:both], o1[both:]], axis=0)
        own_o[head] = o[:, :DIM]
        own_l[head] = o[:, DIM:]
        own_m[head] = jnp.broadcast_to(top, (TOKENS, DIM))

    def own_heads(i, carry):
        for j in range(OWN_UNROLL):
            own_head(i * OWN_UNROLL + j)
        return carry

    lax.fori_loop(0, HEADS // OWN_UNROLL, own_heads, 0)

    lane = iota((GROUP, DIM), 1)

    def guest(head, stat, q, k, v, bias):
        s = dot_nt(q, k) + bias
        top = offset(s)
        o = dot_nn(soft(s, top), with_ones(v))
        for t in range(4):
            rows = slice(t * GROUP, (t + 1) * GROUP)
            stat = jnp.where(lane == 32 * t + head, top[rows], stat)
            stat = jnp.where(lane == 32 * t + HEADS + head, o[rows, DIM:], stat)
        return o[:, :DIM].astype(BF16), stat

    sides = ((0, has_left, left), (1, has_right, right))
    for side, there, device in sides:
        @pl.when(there)
        def _():
            copy_q_flank(side, device).wait_recv()

    stats = [jnp.zeros((GROUP, DIM), F32)] * 2
    for head in range(HEADS):
        at = lanes(head)
        for side in range(2):
            part = pl.ds(side * (TOKENS - FLANK), FLANK)
            k = jnp.concatenate([kv_all[f, part, at] for f in (0, 1, 2, 0)], axis=0)
            v = jnp.concatenate([kv_all[FRAMES + f, part, at] for f in (0, 1, 2, 0)], axis=0)
            o, stats[side] = guest(head, stats[side], q_flank[side, :, at], k, v, bias_flank[side])
            send_o[2 + side, :, at] = o
    for side, there, device in sides:
        send_s[2 + side] = stats[side]

        @pl.when(there)
        def _():
            copy_flank_o(side, device).start()
            copy_flank_s(side, device).start()

    for side, there, device in sides:
        @pl.when(there)
        def _():
            for s in range(2):
                copy_ext(side, s, device).wait_recv()

    def edge_head(side, head, stat):
        at = lanes(head)
        part = pl.ds(pl.multiple_of(side * EDGE, EDGE), EDGE)

        def keys(kv):
            pieces = []
            for f in range(FRAMES):
                pieces.append(kv_pack[kv * FRAMES + f, part, at])
                pieces.append(ext[side, kv * FRAMES + f, :, at])
            return jnp.concatenate(pieces, axis=0)

        o, stat = guest(head, stat, q_edge[side, :, at], keys(0), keys(1), bias_edge[side])
        send_o[side, :, at] = o
        return stat

    def edge_of(turn):
        side = (turn + flip) % 2
        there = jnp.where(side == 0, has_up.astype(jnp.int32), has_down.astype(jnp.int32)) > 0
        return side, there, (h - 1 + 2 * side, w)

    per = HEADS // CHUNKS
    side, there, device = edge_of(0)

    @pl.when(there)
    def _():
        for c in range(CHUNKS):
            copy_q_edge(side, c, device).wait_recv()
        stat = jnp.zeros((GROUP, DIM), F32)
        for head in range(HEADS):
            stat = edge_head(side, head, stat)
        send_s[side] = stat
        for c in range(CHUNKS):
            copy_edge_o(side, c, device).start()
        copy_edge_s(side, device).start()

    side1, there1, device1 = edge_of(1)

    @pl.when(there1)
    def _():
        stat = jnp.zeros((GROUP, DIM), F32)
        for c in range(CHUNKS):
            copy_q_edge(side1, c, device1).wait_recv()
            for i in range(per):
                stat = edge_head(side1, c * per + i, stat)
            copy_edge_o(side1, c, device1).start()
        send_s[side1] = stat
        copy_edge_s(side1, device1).start()

    for side, there, device in sides:
        @pl.when(there)
        def _():
            copy_flank_o(1 - side, device).wait_recv()
            copy_flank_s(1 - side, device).wait_recv()

    def column(stat, index):
        return jnp.concatenate(
            [stat[:, 32 * t + index : 32 * t + index + 1] for t in range(4)], axis=0
        )

    def merge(own, other):
        (m0, l0, o0), (m1, l1, o1) = own, other
        top = jnp.maximum(m0, m1)
        a0, a1 = jnp.exp2(m0 - top), jnp.exp2(m1 - top)
        return top, a0 * l0 + a1 * jnp.maximum(l1, 0.0), a0 * o0 + a1 * o1.astype(F32)

    wide_lane = iota((TOKENS, DIM), 1)
    own_stat = jnp.zeros((TOKENS, DIM), F32)
    for head in range(HEADS):
        at = lanes(head)
        for side in range(2):
            part = pl.ds(side * (TOKENS - FLANK), FLANK)
            stat = flank_s[side]
            top, total, mixed = merge(
                (own_m[head, part], own_l[head, part], own_o[head, part]),
                (column(stat, head), column(stat, HEADS + head), flank_o[side, :, at]),
            )
            own_m[head, part] = top
            own_l[head, part] = total
            own_o[head, part] = mixed
        total = own_l[head]
        high = total.astype(BF16).astype(F32)
        own_stat = jnp.where(wide_lane == head, own_m[head], own_stat)
        own_stat = jnp.where(wide_lane == HEADS + head, high, own_stat)
        own_stat = jnp.where(wide_lane == 2 * HEADS + head, total - high, own_stat)
    packed_stat = dot_nn(pick[...], own_stat.astype(BF16))
    inner = iota((TOKENS, DIM), 0) % ROWS
    inner = (inner >= RADIUS) & (inner < ROWS - RADIUS)
    for head in range(HEADS):
        at = lanes(head)
        o = own_o[head]
        high = o.astype(BF16)
        rest = (o - high.astype(F32)).astype(BF16)
        edge_own_o[head] = dot_nn(pick[...], high) + dot_nn(pick[...], rest)
        edge_own_m[head] = jnp.broadcast_to(packed_stat[:, head : head + 1], (2 * EDGE, DIM))
        edge_own_l[head] = jnp.broadcast_to(
            packed_stat[:, HEADS + head : HEADS + head + 1]
            + packed_stat[:, 2 * HEADS + head : 2 * HEADS + head + 1],
            (2 * EDGE, DIM),
        )
        out[:, at] = jnp.where(inner, o / own_l[head], 0.0).astype(BF16)

    for turn in range(2):
        side, there, device = edge_of(turn)

        @pl.when(there)
        def _():
            for c in range(CHUNKS):
                copy_edge_o(1 - side, c, device).wait_recv()
            copy_edge_s(1 - side, device).wait_recv()

        part = pl.ds(pl.multiple_of(side * EDGE, EDGE), EDGE)
        stat = edge_s[side]
        slot = iota((EDGE, DIM), 0) // RADIUS
        real = (slot < COLS - RADIUS) | (slot >= SLOTS - RADIUS)
        place = jnp.where(side == 0, spread[:, 0:EDGE], spread[:, EDGE : 2 * EDGE])
        for head in range(HEADS):
            at = lanes(head)
            top, total, mixed = merge(
                (edge_own_m[head, part], edge_own_l[head, part], edge_own_o[head, part]),
                (column(stat, head), column(stat, HEADS + head), edge_o[side, :, at]),
            )
            done = jnp.where(real, mixed / total, 0.0).astype(BF16)
            out[:, at] = (out[:, at].astype(F32) + dot_nn(place, done)).astype(BF16)

    for c in range(CHUNKS):
        @pl.when(has_down)
        def _():
            copy_q_edge(0, c, down).wait_send()
            copy_edge_o(1, c, down).wait_send()

        @pl.when(has_up)
        def _():
            copy_q_edge(1, c, up).wait_send()
            copy_edge_o(0, c, up).wait_send()

    @pl.when(has_down)
    def _():
        copy_edge_s(1, down).wait_send()

    @pl.when(has_up)
    def _():
        copy_edge_s(0, up).wait_send()

    for side, there, device in ((0, has_right, right), (1, has_left, left)):
        @pl.when(there)
        def _():
            copy_q_flank(side, device).wait_send()
            for s in range(2):
                copy_ext(side, s, device).wait_send()
            copy_flank_o(1 - side, device).wait_send()
            copy_flank_s(1 - side, device).wait_send()


def on_device(nh, nw, queries, kv_new, kv_past):
    wide = HEADS * DIM
    hbm = pl.BlockSpec(memory_space=pltpu.HBM)
    dma = pltpu.SemaphoreType.DMA
    queries = queries.transpose(1, 0, 2).reshape(TOKENS, wide)
    kv_new = kv_new.transpose(0, 2, 1, 3).reshape(2, TOKENS, wide)
    kv_past = kv_past.transpose(0, 1, 3, 2, 4).reshape(FRAMES - 1, 2, TOKENS, wide)
    out = pl.pallas_call(
        functools.partial(kernel, nh, nw),
        out_shape=jax.ShapeDtypeStruct((TOKENS, wide), BF16),
        in_specs=[hbm] * 3,
        out_specs=pl.BlockSpec(memory_space=pltpu.VMEM),
        scratch_shapes=[
            pltpu.VMEM((TOKENS, wide), BF16),
            pltpu.VMEM((2 * FRAMES, TOKENS, wide), BF16),
            pltpu.VMEM((2 * EDGE, wide), BF16),
            pltpu.VMEM((2 * FRAMES, 2 * EDGE, wide), BF16),
            pltpu.VMEM((2, EDGE, wide), BF16),
            pltpu.VMEM((2, FLANK, wide), BF16),
            pltpu.VMEM((2, 2 * FRAMES, 2 * CORNER, wide), BF16),
            pltpu.VMEM((HEADS, TOKENS, DIM), F32),
            pltpu.VMEM((HEADS, TOKENS, DIM), F32),
            pltpu.VMEM((HEADS, TOKENS, DIM), F32),
            pltpu.VMEM((HEADS, 2 * EDGE, DIM), F32),
            pltpu.VMEM((HEADS, 2 * EDGE, DIM), F32),
            pltpu.VMEM((HEADS, 2 * EDGE, DIM), F32),
            pltpu.VMEM((4, EDGE, wide), BF16),
            pltpu.VMEM((4, GROUP, DIM), F32),
            pltpu.VMEM((2, EDGE, wide), BF16),
            pltpu.VMEM((2, GROUP, DIM), F32),
            pltpu.VMEM((2, FLANK, wide), BF16),
            pltpu.VMEM((2, GROUP, DIM), F32),
            pltpu.VMEM((REACH0, CUT), F32),
            pltpu.VMEM((TOKENS - REACH1, CUT), F32),
            pltpu.VMEM((2, FLANK, (FRAMES + 1) * FLANK), F32),
            pltpu.VMEM((2, EDGE, FRAMES * SPAN), F32),
            pltpu.VMEM((2 * EDGE, TOKENS), BF16),
            pltpu.VMEM((TOKENS, 2 * EDGE), BF16),
            dma((1 + 2 * FRAMES,)),
            dma((2, 2, CHUNKS)),
            dma((2, 2)),
            dma((2, 2, 2)),
            dma((2, 2, CHUNKS)),
            dma((2, 2)),
            dma((2, 4)),
        ],
        compiler_params=pltpu.CompilerParams(
            collective_id=0, has_side_effects=True, vmem_limit_bytes=60 * 1024 * 1024
        ),
    )(queries, kv_new, kv_past)
    return out.reshape(COLS, ROWS, wide).transpose(1, 0, 2)


def solution(mesh):
    return jax.shard_map(
        functools.partial(on_device, mesh.shape["ha"], mesh.shape["wa"]),
        mesh=mesh,
        in_specs=(P("ha", "wa", None), P(None, "ha", "wa", None), P(None, None, "ha", "wa", None)),
        out_specs=P("ha", "wa", None),
        check_vma=False,
    )
```

```python
import functools
import math

import jax
import jax.numpy as jnp
from jax import lax
from jax.experimental import pallas as pl
from jax.experimental.pallas import tpu as pltpu
from jax.sharding import PartitionSpec as P

MESH = pl.DeviceIdType.MESH
HEADS = 8
DIM = 128
RADIUS = 4
FRAMES = 3
ROWS = 16
COLS = 14
TOKENS = ROWS * COLS
FLANK = RADIUS * ROWS
SLOTS = 16
EDGE = SLOTS * RADIUS
CORNER = RADIUS * RADIUS
SPAN = EDGE + 2 * CORNER
CORNERS = 4
GROUP = 16
CHUNKS = 2
LOW = -1e30
VMEM_BYTES = 54579 * 1024
FOLD = math.log2(math.e) / math.sqrt(DIM)
F32 = jnp.float32
BF16 = jnp.bfloat16
CUT = 8 * ROWS
BLOCK1 = TOKENS - CUT
REACH0 = 12 * ROWS
REACH1 = 4 * ROWS
OWN_UNROLL = 8


def dot_nt(a, b):
    return lax.dot_general(a, b, (((1,), (1,)), ((), ())), preferred_element_type=F32)


def dot_nn(a, b):
    return lax.dot_general(a, b, (((1,), (0,)), ((), ())), preferred_element_type=F32)


def iota(shape, dim):
    return lax.broadcasted_iota(jnp.int32, shape, dim)


def lanes(head):
    if isinstance(head, int):
        return pl.ds(head * DIM, DIM)
    return pl.ds(pl.multiple_of(head * DIM, DIM), DIM)


def mask(allowed):
    return jnp.where(allowed, 0.0, LOW)


def edge_col(slot):
    return jnp.where(slot < COLS - RADIUS, slot, slot - (SLOTS - COLS))


def soft(scores, top):
    return jnp.exp2(scores * FOLD - top).astype(BF16)


def with_ones(values):
    return jnp.concatenate([values, jnp.ones_like(values)], axis=1)


def offset(scores):
    top = FOLD * jnp.max(scores, axis=1, keepdims=True)
    return top.astype(BF16).astype(F32)


def kernel(
    nh, nw,
    q_hbm, new_hbm, past_hbm, out,
    q_all, kv_all, q_pack, kv_pack,
    q_edge, q_flank, q_corner, ext, own_o, own_m, own_l, edge_own_o, edge_own_m, edge_own_l,
    send_o, send_s, edge_o, edge_s, flank_o, flank_s, corner_o, corner_s,
    via_q, via_o, via_s,
    bias0, bias1, bias_flank, bias_near, bias_far, bias_corner, pick, spread,
    load_sem, q_edge_sem, q_flank_sem, q_corner_sem, ext_sem,
    edge_sem, flank_sem, corner_sem, stat_sem, via_sem, onward_sem,
):
    h = lax.axis_index("ha")
    w = lax.axis_index("wa")
    has_up, has_down = h > 0, h < nh - 1
    has_left, has_right = w > 0, w < nw - 1
    up, down = (h - 1, w), (h + 1, w)
    left, right = (h, w - 1), (h, w + 1)
    flip = (h == nh // 2).astype(jnp.int32)
    far_up, far_down = h == nh // 2, h == nh // 2 - 1
    far = far_up | far_down
    near_up, near_down = has_up & (h != nh // 2), has_down & (h != nh // 2 - 1)
    corners = (
        (near_up & has_left, (h - 1, w - 1)),
        (near_up & has_right, (h - 1, w + 1)),
        (near_down & has_left, (h + 1, w - 1)),
        (near_down & has_right, (h + 1, w + 1)),
    )
    near = ((near_up, up), (near_down, down), (has_left, left), (has_right, right)) + corners

    relayed = (w >= nw // 2) & ((w // 4 - nw // 8) % 2 == 1)
    via_down, via_up = nh // 2 + 2, nh // 2 - 3
    serves_down, serves_up = relayed & (h == via_down), relayed & (h == via_up)
    serves = serves_down | serves_up
    far_side = serves_up.astype(jnp.int32)
    served, target = (nh // 2 - 1 + far_side, w), (nh // 2 - far_side, w)
    my_via = (jnp.where(far_down, via_down, via_up), w)
    other_via = (jnp.where(far_down, via_up, via_down), w)
    far_via, far_direct = far & relayed, far & jnp.logical_not(relayed)
    across = (nh // 2 - flip, w)
    greet = near + ((far_via, other_via), (far_direct, across), (serves, served))
    awaited = [there for there, _ in near] + [far, serves]

    barrier = pltpu.get_barrier_semaphore()
    for there, device in greet:
        @pl.when(there)
        def _():
            pl.semaphore_signal(barrier, inc=1, device_id=device, device_id_type=MESH)

    loads = [pltpu.make_async_copy(q_hbm, q_all, load_sem.at[0])]
    for kv in range(2):
        for f in range(FRAMES):
            source = new_hbm.at[kv] if f == FRAMES - 1 else past_hbm.at[f, kv]
            slot = kv * FRAMES + f
            loads.append(pltpu.make_async_copy(source, kv_all.at[slot], load_sem.at[1 + slot]))
    for load in loads:
        load.start()

    def picked(shape, dim):
        i, t = iota(shape, dim), iota(shape, 1 - dim)
        slot = i % EDGE // RADIUS
        real = (slot < COLS - RADIUS) | (slot >= SLOTS - RADIUS)
        token = edge_col(slot) * ROWS + i % RADIUS + i // EDGE * (ROWS - RADIUS)
        return jnp.where(real & (t == token), 1.0, 0.0).astype(BF16)

    pick[...] = picked((2 * EDGE, TOKENS), 0)
    spread[...] = picked((TOKENS, 2 * EDGE), 1)

    for there, side in ((has_up, 0), (has_down, 1)):
        @pl.when(jnp.logical_not(there))
        def _():
            q_edge[side] = jnp.zeros(q_edge.shape[1:], BF16)
            edge_o[side] = jnp.zeros(edge_o.shape[1:], BF16)
            edge_s[side] = jnp.full(edge_s.shape[1:], LOW, F32)
    for there, side in ((has_left, 0), (has_right, 1)):
        @pl.when(jnp.logical_not(there))
        def _():
            q_flank[side] = jnp.zeros(q_flank.shape[1:], BF16)
            flank_o[side] = jnp.zeros(flank_o.shape[1:], BF16)
            flank_s[side] = jnp.full(flank_s.shape[1:], LOW, F32)

        @pl.when(jnp.logical_not(there & far))
        def _():
            ext[:, side * CORNER : (side + 1) * CORNER, :] = jnp.zeros(
                (2 * FRAMES, CORNER, HEADS * DIM), BF16
            )
    for t, (there, _) in enumerate(corners):
        @pl.when(jnp.logical_not(there))
        def _():
            rows = slice(t * CORNER, (t + 1) * CORNER)
            q_corner[rows, :] = jnp.zeros((CORNER, HEADS * DIM), BF16)
            corner_o[rows, :] = jnp.zeros((CORNER, HEADS * DIM), BF16)
            corner_s[t] = jnp.full(corner_s.shape[1:], LOW, F32)

    loads[0].wait()
    q_pack[...] = dot_nn(pick[...], q_all[...]).astype(BF16)

    def remote(src, dst, sems, index, device):
        return pltpu.make_async_remote_copy(
            src_ref=src,
            dst_ref=dst,
            send_sem=sems.at[(0, *index)],
            recv_sem=sems.at[(1, *index)],
            device_id=device,
            device_id_type=MESH,
        )

    width = HEADS * DIM // CHUNKS

    def copy_q_edge(side, c, device):
        part = pl.ds(c * width, width)
        return remote(
            q_pack.at[pl.ds((1 - side) * EDGE, EDGE), part],
            q_edge.at[side, :, part],
            q_edge_sem,
            (side, c),
            device,
        )

    def copy_q_flank(side, device):
        return remote(
            q_all.at[pl.ds((1 - side) * (TOKENS - FLANK), FLANK)],
            q_flank.at[side],
            q_flank_sem,
            (side,),
            device,
        )

    def corner_rows(t):
        return pl.ds(t // 2 * EDGE + t % 2 * (EDGE - CORNER), CORNER)

    def copy_q_corner(t, device):
        return remote(
            q_pack.at[corner_rows(t)],
            q_corner.at[pl.ds((CORNERS - 1 - t) * CORNER, CORNER)],
            q_corner_sem,
            (CORNERS - 1 - t,),
            device,
        )

    def copy_ext(side, device):
        start = (1 - side) * (EDGE - CORNER) + (1 - flip) * EDGE
        return remote(
            kv_pack.at[:, pl.ds(pl.multiple_of(start, CORNER), CORNER)],
            ext.at[:, pl.ds(side * CORNER, CORNER)],
            ext_sem,
            (side,),
            device,
        )

    def copy_edge_o(side, c, device):
        part = pl.ds(c * width, width)
        return remote(
            send_o.at[side, :, part],
            edge_o.at[1 - side, :, part],
            edge_sem,
            (1 - side, c),
            device,
        )

    def copy_edge_s(side, device):
        return remote(send_s.at[side], edge_s.at[1 - side], stat_sem, (1 - side,), device)

    def copy_flank_o(side, device):
        return remote(send_o.at[2 + side], flank_o.at[1 - side], flank_sem, (1 - side,), device)

    def copy_flank_s(side, device):
        return remote(send_s.at[2 + side], flank_s.at[1 - side], stat_sem, (3 - side,), device)

    def copy_corner_o(t, device):
        return remote(
            send_o.at[4, pl.ds(t * CORNER, CORNER)],
            corner_o.at[pl.ds((CORNERS - 1 - t) * CORNER, CORNER)],
            corner_sem,
            (CORNERS - 1 - t,),
            device,
        )

    def copy_corner_s(t, device):
        return remote(
            send_s.at[4], corner_s.at[CORNERS - 1 - t], stat_sem, (7 - t,), device
        )

    def to_via(src, dst, index):
        return remote(src, dst, via_sem, (index,), my_via)

    def onward(src, dst, index, there_sem):
        return pltpu.make_async_remote_copy(
            src_ref=src,
            dst_ref=dst,
            send_sem=onward_sem.at[index],
            recv_sem=there_sem,
            device_id=target,
            device_id_type=MESH,
        )

    def to_via_q(c):
        part = pl.ds(c * width, width)
        start = pl.multiple_of((1 - flip) * EDGE, EDGE)
        return to_via(q_pack.at[pl.ds(start, EDGE), part], via_q.at[:, part], c)

    def far_q(c):
        part = pl.ds(c * width, width)
        start = pl.multiple_of((1 - flip) * EDGE, EDGE)
        return remote(
            q_pack.at[pl.ds(start, EDGE), part],
            q_edge.at[flip, :, part],
            q_edge_sem,
            (flip, c),
            across,
        )

    def to_via_o(c):
        part = pl.ds(c * width, width)
        return to_via(send_o.at[1 - flip, :, part], via_o.at[:, part], CHUNKS + c)

    def to_via_s():
        return to_via(send_s.at[1 - flip], via_s, 2 * CHUNKS)

    def onward_q(c):
        part = pl.ds(c * width, width)
        return onward(
            via_q.at[:, part], q_edge.at[far_side, :, part], c, q_edge_sem.at[1, far_side, c]
        )

    def onward_o(c):
        part = pl.ds(c * width, width)
        return onward(
            via_o.at[:, part], edge_o.at[far_side, :, part], CHUNKS + c, edge_sem.at[1, far_side, c]
        )

    def onward_s():
        return onward(via_s, edge_s.at[far_side], 2 * CHUNKS, stat_sem.at[1, far_side])

    pl.semaphore_wait(barrier, sum(there.astype(jnp.int32) for there in awaited))

    for c in range(CHUNKS):
        @pl.when(far_via)
        def _():
            to_via_q(c).start()

        @pl.when(far_direct)
        def _():
            far_q(c).start()

        @pl.when(near_down)
        def _():
            copy_q_edge(0, c, down).start()

        @pl.when(near_up)
        def _():
            copy_q_edge(1, c, up).start()

    @pl.when(has_right)
    def _():
        copy_q_flank(0, right).start()

    @pl.when(has_left)
    def _():
        copy_q_flank(1, left).start()

    for t, (there, device) in enumerate(corners):
        @pl.when(there)
        def _():
            copy_q_corner(t, device).start()

    for slot in range(2 * FRAMES):
        loads[1 + slot].wait()
        kv_pack[slot] = dot_nn(pick[...], kv_all[slot]).astype(BF16)

    @pl.when(far & has_right)
    def _():
        copy_ext(0, right).start()

    @pl.when(far & has_left)
    def _():
        copy_ext(1, left).start()

    q, k = iota(bias0.shape, 0), iota(bias0.shape, 1)
    bias0[...] = mask((abs(q // ROWS - k // ROWS) <= RADIUS) & (abs(q % ROWS - k % ROWS) <= RADIUS))
    q, k = iota(bias1.shape, 0) + REACH1, iota(bias1.shape, 1) + BLOCK1
    bias1[...] = mask(
        (abs(q // ROWS - k // ROWS) <= RADIUS) & (abs(q % ROWS - k % ROWS) <= RADIUS) & (k >= CUT)
    )

    q, k = iota(bias_flank.shape[1:], 0), iota(bias_flank.shape[1:], 1)
    rows_near = (abs(q % ROWS - k % ROWS) <= RADIUS) & (k < FRAMES * FLANK)
    k = k % FLANK
    bias_flank[0] = mask(rows_near & (k // ROWS <= q // ROWS))
    bias_flank[1] = mask(rows_near & (k // ROWS >= q // ROWS))

    def real_slot(slot):
        return (slot < COLS - RADIUS) | (slot >= SLOTS - RADIUS)

    q, k = iota(bias_near.shape[1:], 0), iota(bias_near.shape[1:], 1)
    slot = k % EDGE // RADIUS
    cols_near = abs(edge_col(q // RADIUS) - edge_col(slot)) <= RADIUS
    cols_near = cols_near & real_slot(slot) & (k < FRAMES * EDGE)
    bias_near[0] = mask(cols_near & (k % RADIUS <= q % RADIUS))
    bias_near[1] = mask(cols_near & (k % RADIUS >= q % RADIUS))

    q, k = iota(bias_far.shape, 0), iota(bias_far.shape, 1) % SPAN
    slot = k // RADIUS
    in_left = (k >= EDGE) & (k < EDGE + CORNER)
    in_right = k >= EDGE + CORNER
    key_col = jnp.where(
        in_left, slot - SLOTS - RADIUS, jnp.where(in_right, slot - SLOTS - RADIUS + COLS, edge_col(slot))
    )
    real = jnp.where(
        in_left,
        (far & has_left).astype(jnp.int32),
        jnp.where(in_right, (far & has_right).astype(jnp.int32), real_slot(slot).astype(jnp.int32)),
    )
    sign = 2 * flip - 1
    rows_near = (q % RADIUS - k % RADIUS) * sign >= 0
    bias_far[...] = mask((abs(edge_col(q // RADIUS) - key_col) <= RADIUS) & (real > 0) & rows_near)

    q, k = iota(bias_corner.shape, 0), iota(bias_corner.shape, 1)
    same = (q // CORNER == k % EDGE // CORNER) & (k < FRAMES * EDGE)
    down_sign, right_sign = 1 - q // CORNER // 2 * 2, 1 - q // CORNER % 2 * 2
    rows_near = (q % RADIUS - k % RADIUS) * down_sign >= 0
    cols_near = (q % CORNER // RADIUS - k % CORNER // RADIUS) * right_sign >= 0
    bias_corner[...] = mask(same & rows_near & cols_near)

    def own_head(head):
        at = lanes(head)

        def block(kv, first, size):
            return jnp.concatenate(
                [kv_all[kv * FRAMES + f, pl.ds(first, size), at] for f in range(FRAMES)], axis=0
            )

        s0 = dot_nt(q_all[0:REACH0, at], block(0, 0, CUT)) + jnp.concatenate(
            [bias0[...]] * FRAMES, axis=1
        )
        s1 = dot_nt(q_all[REACH1:TOKENS, at], block(0, BLOCK1, CUT)) + jnp.concatenate(
            [bias1[...]] * FRAMES, axis=1
        )
        t0 = jnp.max(s0, axis=1, keepdims=True)
        t1 = jnp.max(s1, axis=1, keepdims=True)
        both = REACH0 - REACH1
        top = FOLD * jnp.concatenate(
            [t0[0:REACH1], jnp.maximum(t0[REACH1:], t1[0:both]), t1[both:]], axis=0
        )
        top = top.astype(BF16).astype(F32)
        o0 = dot_nn(soft(s0, top[0:REACH0]), with_ones(block(1, 0, CUT)))
        o1 = dot_nn(soft(s1, top[REACH1:TOKENS]), with_ones(block(1, BLOCK1, CUT)))
        o = jnp.concatenate([o0[0:REACH1], o0[REACH1:] + o1[0:both], o1[both:]], axis=0)
        own_o[head] = o[:, :DIM]
        own_l[head] = o[:, DIM:]
        own_m[head] = jnp.broadcast_to(top, (TOKENS, DIM))

    def own_heads(i, carry):
        for j in range(OWN_UNROLL):
            own_head(i * OWN_UNROLL + j)
        return carry

    lax.fori_loop(0, HEADS // OWN_UNROLL, own_heads, 0)

    lane = iota((GROUP, DIM), 1)

    def guest(head, stat, q, k, v, bias):
        s = dot_nt(q, k) + bias
        top = offset(s)
        o = dot_nn(soft(s, top), with_ones(v))
        for t in range(4):
            rows = slice(t * GROUP, (t + 1) * GROUP)
            stat = jnp.where(lane == 32 * t + head, top[rows], stat)
            stat = jnp.where(lane == 32 * t + HEADS + head, o[rows, DIM:], stat)
        return o[:, :DIM].astype(BF16), stat

    sides = ((0, has_left, left), (1, has_right, right))
    for side, there, device in sides:
        @pl.when(there)
        def _():
            copy_q_flank(side, device).wait_recv()

    stats = [jnp.zeros((GROUP, DIM), F32)] * 2
    for head in range(HEADS):
        at = lanes(head)
        for side in range(2):
            part = pl.ds(side * (TOKENS - FLANK), FLANK)
            k = jnp.concatenate([kv_all[f, part, at] for f in (0, 1, 2, 0)], axis=0)
            v = jnp.concatenate([kv_all[FRAMES + f, part, at] for f in (0, 1, 2, 0)], axis=0)
            o, stats[side] = guest(head, stats[side], q_flank[side, :, at], k, v, bias_flank[side])
            send_o[2 + side, :, at] = o
    for side, there, device in sides:
        send_s[2 + side] = stats[side]

        @pl.when(there)
        def _():
            copy_flank_o(side, device).start()
            copy_flank_s(side, device).start()

    def near_head(side, head, stat):
        at = lanes(head)
        part = pl.ds(pl.multiple_of(side * EDGE, EDGE), EDGE)
        k = jnp.concatenate([kv_pack[f, part, at] for f in (0, 1, 2, 0)], axis=0)
        v = jnp.concatenate([kv_pack[FRAMES + f, part, at] for f in (0, 1, 2, 0)], axis=0)
        o, stat = guest(head, stat, q_edge[side, :, at], k, v, bias_near[side])
        send_o[side, :, at] = o
        return stat

    def far_head(side, head, stat):
        at = lanes(head)
        part = pl.ds(pl.multiple_of(side * EDGE, EDGE), EDGE)

        def keys(kv):
            pieces = []
            for f in range(FRAMES):
                pieces.append(kv_pack[kv * FRAMES + f, part, at])
                pieces.append(ext[kv * FRAMES + f, :, at])
            return jnp.concatenate(pieces, axis=0)

        o, stat = guest(head, stat, q_edge[side, :, at], keys(0), keys(1), bias_far[...])
        send_o[side, :, at] = o
        return stat

    def edge_of(turn):
        side = (turn + flip) % 2
        there = jnp.where(side == 0, has_up.astype(jnp.int32), has_down.astype(jnp.int32)) > 0
        return side, there, (h - 1 + 2 * side, w)

    per = HEADS // CHUNKS
    side, there, device = edge_of(0)

    @pl.when(there)
    def _():
        for c in range(CHUNKS):
            copy_q_edge(side, c, device).wait_recv()
        stat = jnp.zeros((GROUP, DIM), F32)
        for head in range(HEADS):
            stat = near_head(side, head, stat)
        send_s[side] = stat
        for c in range(CHUNKS):
            copy_edge_o(side, c, device).start()
        copy_edge_s(side, device).start()

    for t, (there, device) in enumerate(corners):
        @pl.when(there)
        def _():
            copy_q_corner(CORNERS - 1 - t, device).wait_recv()

    stat = jnp.zeros((GROUP, DIM), F32)
    for head in range(HEADS):
        at = lanes(head)

        def corner_keys(kv):
            pieces = []
            for f in (0, 1, 2, 0):
                for t in range(CORNERS):
                    pieces.append(kv_pack[kv * FRAMES + f, corner_rows(t), at])
            return jnp.concatenate(pieces, axis=0)

        o, stat = guest(
            head, stat, q_corner[:, at], corner_keys(0), corner_keys(1), bias_corner[...]
        )
        send_o[4, :, at] = o
    send_s[4] = stat
    for t, (there, device) in enumerate(corners):
        @pl.when(there)
        def _():
            copy_corner_o(t, device).start()
            copy_corner_s(t, device).start()

    for side, there, device in sides:
        @pl.when(there & far)
        def _():
            copy_ext(side, device).wait_recv()

    side1, there1, device1 = edge_of(1)

    @pl.when(there1)
    def _():
        stat = jnp.zeros((GROUP, DIM), F32)
        for c in range(CHUNKS):
            copy_q_edge(side1, c, device1).wait_recv()
            for i in range(per):
                stat = far_head(side1, c * per + i, stat)

            @pl.when(far_via)
            def _():
                to_via_o(c).start()

            @pl.when(jnp.logical_not(far_via))
            def _():
                copy_edge_o(side1, c, device1).start()

        send_s[side1] = stat

        @pl.when(far_via)
        def _():
            to_via_s().start()

        @pl.when(jnp.logical_not(far_via))
        def _():
            copy_edge_s(side1, device1).start()

    @pl.when(serves)
    def _():
        for c in range(CHUNKS):
            to_via_q(c).wait_recv()
            onward_q(c).start()

    for side, there, device in sides:
        @pl.when(there)
        def _():
            copy_flank_o(1 - side, device).wait_recv()
            copy_flank_s(1 - side, device).wait_recv()

    def column(stat, index):
        return jnp.concatenate(
            [stat[:, 32 * t + index : 32 * t + index + 1] for t in range(4)], axis=0
        )

    def merge(own, other):
        (m0, l0, o0), (m1, l1, o1) = own, other
        top = jnp.maximum(m0, m1)
        a0, a1 = jnp.exp2(m0 - top), jnp.exp2(m1 - top)
        return top, a0 * l0 + a1 * jnp.maximum(l1, 0.0), a0 * o0 + a1 * o1.astype(F32)

    wide_lane = iota((TOKENS, DIM), 1)
    own_stat = jnp.zeros((TOKENS, DIM), F32)
    for head in range(HEADS):
        at = lanes(head)
        for side in range(2):
            part = pl.ds(side * (TOKENS - FLANK), FLANK)
            stat = flank_s[side]
            top, total, mixed = merge(
                (own_m[head, part], own_l[head, part], own_o[head, part]),
                (column(stat, head), column(stat, HEADS + head), flank_o[side, :, at]),
            )
            own_m[head, part] = top
            own_l[head, part] = total
            own_o[head, part] = mixed
        total = own_l[head]
        high = total.astype(BF16).astype(F32)
        own_stat = jnp.where(wide_lane == head, own_m[head], own_stat)
        own_stat = jnp.where(wide_lane == HEADS + head, high, own_stat)
        own_stat = jnp.where(wide_lane == 2 * HEADS + head, total - high, own_stat)
    packed_stat = dot_nn(pick[...], own_stat.astype(BF16))
    inner = iota((TOKENS, DIM), 0) % ROWS
    inner = (inner >= RADIUS) & (inner < ROWS - RADIUS)
    for head in range(HEADS):
        at = lanes(head)
        o = own_o[head]
        high = o.astype(BF16)
        rest = (o - high.astype(F32)).astype(BF16)
        edge_own_o[head] = dot_nn(pick[...], high) + dot_nn(pick[...], rest)
        edge_own_m[head] = jnp.broadcast_to(packed_stat[:, head : head + 1], (2 * EDGE, DIM))
        edge_own_l[head] = jnp.broadcast_to(
            packed_stat[:, HEADS + head : HEADS + head + 1]
            + packed_stat[:, 2 * HEADS + head : 2 * HEADS + head + 1],
            (2 * EDGE, DIM),
        )
        out[:, at] = jnp.where(inner, o / own_l[head], 0.0).astype(BF16)

    for t, (there, device) in enumerate(corners):
        @pl.when(there)
        def _():
            copy_corner_o(CORNERS - 1 - t, device).wait_recv()
            copy_corner_s(CORNERS - 1 - t, device).wait_recv()

    slot = iota((EDGE, DIM), 0) // RADIUS
    real = real_slot(slot)
    for side in range(2):
        for lr in range(2):
            t = 2 * side + lr
            part = pl.ds(side * EDGE + lr * (EDGE - CORNER), CORNER)
            first = 32 * (CORNERS - 1 - t)
            stat = corner_s[t]
            for head in range(HEADS):
                m1 = stat[:, first + head : first + head + 1]
                l1 = stat[:, first + HEADS + head : first + HEADS + head + 1]
                o1 = corner_o[t * CORNER : (t + 1) * CORNER, lanes(head)]
                top, total, mixed = merge(
                    (edge_own_m[head, part], edge_own_l[head, part], edge_own_o[head, part]),
                    (m1, l1, o1),
                )
                edge_own_m[head, part] = top
                edge_own_l[head, part] = total
                edge_own_o[head, part] = mixed

    for turn in range(2):
        side, there, device = edge_of(turn)
        part = pl.ds(pl.multiple_of(side * EDGE, EDGE), EDGE)
        place = jnp.where(side == 0, spread[:, 0:EDGE], spread[:, EDGE : 2 * EDGE])

        @pl.when(there)
        def _():
            for c in range(CHUNKS):
                copy_edge_o(1 - side, c, device).wait_recv()
            copy_edge_s(1 - side, device).wait_recv()

        stat = edge_s[side]
        for head in range(HEADS):
            at = lanes(head)
            top, total, mixed = merge(
                (edge_own_m[head, part], edge_own_l[head, part], edge_own_o[head, part]),
                (column(stat, head), column(stat, HEADS + head), edge_o[side, :, at]),
            )
            done = jnp.where(real, mixed / total, 0.0).astype(BF16)
            out[:, at] = out[:, at] + dot_nn(place, done).astype(BF16)

    @pl.when(serves)
    def _():
        for c in range(CHUNKS):
            to_via_o(c).wait_recv()
            onward_o(c).start()
        to_via_s().wait_recv()
        onward_s().start()
        for c in range(CHUNKS):
            onward_q(c).wait_send()
            onward_o(c).wait_send()
        onward_s().wait_send()

    @pl.when(far_via)
    def _():
        for c in range(CHUNKS):
            to_via_q(c).wait_send()
            to_via_o(c).wait_send()
        to_via_s().wait_send()

    @pl.when(far_direct)
    def _():
        for c in range(CHUNKS):
            far_q(c).wait_send()
            copy_edge_o(side1, c, device1).wait_send()
        copy_edge_s(side1, device1).wait_send()

    for c in range(CHUNKS):
        @pl.when(near_down)
        def _():
            copy_q_edge(0, c, down).wait_send()
            copy_edge_o(1, c, down).wait_send()

        @pl.when(near_up)
        def _():
            copy_q_edge(1, c, up).wait_send()
            copy_edge_o(0, c, up).wait_send()

    @pl.when(near_down)
    def _():
        copy_edge_s(1, down).wait_send()

    @pl.when(near_up)
    def _():
        copy_edge_s(0, up).wait_send()

    for side, there, device in ((0, has_right, right), (1, has_left, left)):
        @pl.when(there)
        def _():
            copy_q_flank(side, device).wait_send()
            copy_flank_o(1 - side, device).wait_send()
            copy_flank_s(1 - side, device).wait_send()

        @pl.when(there & far)
        def _():
            copy_ext(side, device).wait_send()

    for t, (there, device) in enumerate(corners):
        @pl.when(there)
        def _():
            copy_q_corner(t, device).wait_send()
            copy_corner_o(t, device).wait_send()
            copy_corner_s(t, device).wait_send()


def on_device(nh, nw, queries, kv_new, kv_past):
    wide = HEADS * DIM
    hbm = pl.BlockSpec(memory_space=pltpu.HBM)
    dma = pltpu.SemaphoreType.DMA
    queries = queries.transpose(1, 0, 2).reshape(TOKENS, wide)
    kv_new = kv_new.transpose(0, 2, 1, 3).reshape(2, TOKENS, wide)
    kv_past = kv_past.transpose(0, 1, 3, 2, 4).reshape(FRAMES - 1, 2, TOKENS, wide)
    out = pl.pallas_call(
        functools.partial(kernel, nh, nw),
        out_shape=jax.ShapeDtypeStruct((TOKENS, wide), BF16),
        in_specs=[hbm] * 3,
        out_specs=pl.BlockSpec(memory_space=pltpu.VMEM),
        scratch_shapes=[
            pltpu.VMEM((TOKENS, wide), BF16),
            pltpu.VMEM((2 * FRAMES, TOKENS, wide), BF16),
            pltpu.VMEM((2 * EDGE, wide), BF16),
            pltpu.VMEM((2 * FRAMES, 2 * EDGE, wide), BF16),
            pltpu.VMEM((2, EDGE, wide), BF16),
            pltpu.VMEM((2, FLANK, wide), BF16),
            pltpu.VMEM((CORNERS * CORNER, wide), BF16),
            pltpu.VMEM((2 * FRAMES, 2 * CORNER, wide), BF16),
            pltpu.VMEM((HEADS, TOKENS, DIM), F32),
            pltpu.VMEM((HEADS, TOKENS, DIM), F32),
            pltpu.VMEM((HEADS, TOKENS, DIM), F32),
            pltpu.VMEM((HEADS, 2 * EDGE, DIM), F32),
            pltpu.VMEM((HEADS, 2 * EDGE, DIM), F32),
            pltpu.VMEM((HEADS, 2 * EDGE, DIM), F32),
            pltpu.VMEM((5, EDGE, wide), BF16),
            pltpu.VMEM((5, GROUP, DIM), F32),
            pltpu.VMEM((2, EDGE, wide), BF16),
            pltpu.VMEM((2, GROUP, DIM), F32),
            pltpu.VMEM((2, FLANK, wide), BF16),
            pltpu.VMEM((2, GROUP, DIM), F32),
            pltpu.VMEM((CORNERS * CORNER, wide), BF16),
            pltpu.VMEM((CORNERS, GROUP, DIM), F32),
            pltpu.VMEM((EDGE, wide), BF16),
            pltpu.VMEM((EDGE, wide), BF16),
            pltpu.VMEM((GROUP, DIM), F32),
            pltpu.VMEM((REACH0, CUT), F32),
            pltpu.VMEM((TOKENS - REACH1, CUT), F32),
            pltpu.VMEM((2, FLANK, (FRAMES + 1) * FLANK), F32),
            pltpu.VMEM((2, EDGE, (FRAMES + 1) * EDGE), F32),
            pltpu.VMEM((EDGE, FRAMES * SPAN), F32),
            pltpu.VMEM((EDGE, (FRAMES + 1) * EDGE), F32),
            pltpu.VMEM((2 * EDGE, TOKENS), BF16),
            pltpu.VMEM((TOKENS, 2 * EDGE), BF16),
            dma((1 + 2 * FRAMES,)),
            dma((2, 2, CHUNKS)),
            dma((2, 2)),
            dma((2, CORNERS)),
            dma((2, 2)),
            dma((2, 2, CHUNKS)),
            dma((2, 2)),
            dma((2, CORNERS)),
            dma((2, 8)),
            dma((2, 2 * CHUNKS + 1)),
            dma((2 * CHUNKS + 1,)),
        ],
        compiler_params=pltpu.CompilerParams(
            collective_id=0, has_side_effects=True, vmem_limit_bytes=VMEM_BYTES
        ),
    )(queries, kv_new, kv_past)
    return out.reshape(COLS, ROWS, wide).transpose(1, 0, 2)


def solution(mesh):
    return jax.shard_map(
        functools.partial(on_device, mesh.shape["ha"], mesh.shape["wa"]),
        mesh=mesh,
        in_specs=(P("ha", "wa", None), P(None, "ha", "wa", None), P(None, None, "ha", "wa", None)),
        out_specs=P("ha", "wa", None),
        check_vma=False,
    )
```

```python
import functools
import math

import jax
import jax.numpy as jnp
from jax import lax
from jax.experimental import pallas as pl
from jax.experimental.pallas import tpu as pltpu
from jax.sharding import PartitionSpec as P

MESH = pl.DeviceIdType.MESH
HEADS = 8
DIM = 128
RADIUS = 4
FRAMES = 3
ROWS = 16
COLS = 14
TOKENS = ROWS * COLS
FLANK = RADIUS * ROWS
SLOTS = 16
EDGE = SLOTS * RADIUS
CORNER = RADIUS * RADIUS
SPAN = EDGE + 2 * CORNER
CORNERS = 4
GROUP = 16
CHUNKS = 2
LOW = -1e30
VMEM_BYTES = 54579 * 1024
FOLD = math.log2(math.e) / math.sqrt(DIM)
F32 = jnp.float32
BF16 = jnp.bfloat16
CUT = 8 * ROWS
BLOCK1 = TOKENS - CUT
REACH0 = 12 * ROWS
REACH1 = 4 * ROWS
OWN_UNROLL = 2


def dot_nt(a, b):
    return lax.dot_general(a, b, (((1,), (1,)), ((), ())), preferred_element_type=F32)


def dot_nn(a, b):
    return lax.dot_general(a, b, (((1,), (0,)), ((), ())), preferred_element_type=F32)


def iota(shape, dim):
    return lax.broadcasted_iota(jnp.int32, shape, dim)


def lanes(head):
    if isinstance(head, int):
        return pl.ds(head * DIM, DIM)
    return pl.ds(pl.multiple_of(head * DIM, DIM), DIM)


def mask(allowed):
    return jnp.where(allowed, 0.0, LOW)


def edge_col(slot):
    return jnp.where(slot < COLS - RADIUS, slot, slot - (SLOTS - COLS))


def soft(scores, top):
    return jnp.exp2(scores * FOLD - top).astype(BF16)


def with_ones(values):
    return jnp.concatenate([values, jnp.ones_like(values)], axis=1)


def offset(scores):
    top = FOLD * jnp.max(scores, axis=1, keepdims=True)
    return top.astype(BF16).astype(F32)


def kernel(
    nh, nw,
    q_hbm, new_hbm, past_hbm, out,
    q_all, kv_all, q_pack, kv_pack,
    q_edge, q_flank, q_corner, ext, own_o, own_m, own_l, edge_own_o, edge_own_m, edge_own_l,
    send_o, send_s, edge_o, edge_s, flank_o, flank_s, corner_o, corner_s,
    via_q, via_o, via_s,
    bias0, bias1, bias_flank, bias_near, bias_far, bias_corner, pick, spread,
    load_sem, q_edge_sem, q_flank_sem, q_corner_sem, ext_sem,
    edge_sem, flank_sem, corner_sem, stat_sem, via_sem, onward_sem,
):
    h = lax.axis_index("ha")
    w = lax.axis_index("wa")
    has_up, has_down = h > 0, h < nh - 1
    has_left, has_right = w > 0, w < nw - 1
    up, down = (h - 1, w), (h + 1, w)
    left, right = (h, w - 1), (h, w + 1)
    flip = (h == nh // 2).astype(jnp.int32)
    far_up, far_down = h == nh // 2, h == nh // 2 - 1
    far = far_up | far_down
    near_up, near_down = has_up & (h != nh // 2), has_down & (h != nh // 2 - 1)
    corners = (
        (near_up & has_left, (h - 1, w - 1)),
        (near_up & has_right, (h - 1, w + 1)),
        (near_down & has_left, (h + 1, w - 1)),
        (near_down & has_right, (h + 1, w + 1)),
    )
    near = ((near_up, up), (near_down, down), (has_left, left), (has_right, right)) + corners

    relayed = (w >= nw // 2) & ((w // 4 - nw // 8) % 2 == 1)
    via_down, via_up = nh // 2 + 2, nh // 2 - 3
    serves_down, serves_up = relayed & (h == via_down), relayed & (h == via_up)
    serves = serves_down | serves_up
    far_side = serves_up.astype(jnp.int32)
    served, target = (nh // 2 - 1 + far_side, w), (nh // 2 - far_side, w)
    my_via = (jnp.where(far_down, via_down, via_up), w)
    other_via = (jnp.where(far_down, via_up, via_down), w)
    far_via, far_direct = far & relayed, far & jnp.logical_not(relayed)
    across = (nh // 2 - flip, w)
    patient = far_down & far_direct & (w // 4 == nw // 8 - 1)
    greet = near + ((far_via, other_via), (far_direct, across), (serves, served))
    awaited = [there for there, _ in near] + [far, serves]

    barrier = pltpu.get_barrier_semaphore()
    for there, device in greet:
        @pl.when(there)
        def _():
            pl.semaphore_signal(barrier, inc=1, device_id=device, device_id_type=MESH)

    loads = [pltpu.make_async_copy(q_hbm, q_all, load_sem.at[0])]
    for kv in range(2):
        for f in range(FRAMES):
            source = new_hbm.at[kv] if f == FRAMES - 1 else past_hbm.at[f, kv]
            slot = kv * FRAMES + f
            loads.append(pltpu.make_async_copy(source, kv_all.at[slot], load_sem.at[1 + slot]))
    for load in loads:
        load.start()

    def picked(shape, dim):
        i, t = iota(shape, dim), iota(shape, 1 - dim)
        slot = i % EDGE // RADIUS
        real = (slot < COLS - RADIUS) | (slot >= SLOTS - RADIUS)
        token = edge_col(slot) * ROWS + i % RADIUS + i // EDGE * (ROWS - RADIUS)
        return jnp.where(real & (t == token), 1.0, 0.0).astype(BF16)

    pick[...] = picked((2 * EDGE, TOKENS), 0)
    spread[...] = picked((TOKENS, 2 * EDGE), 1)

    for there, side in ((has_up, 0), (has_down, 1)):
        @pl.when(jnp.logical_not(there))
        def _():
            q_edge[side] = jnp.zeros(q_edge.shape[1:], BF16)
            edge_o[side] = jnp.zeros(edge_o.shape[1:], BF16)
            edge_s[side] = jnp.full(edge_s.shape[1:], LOW, F32)
    for there, side in ((has_left, 0), (has_right, 1)):
        @pl.when(jnp.logical_not(there))
        def _():
            q_flank[side] = jnp.zeros(q_flank.shape[1:], BF16)
            flank_o[side] = jnp.zeros(flank_o.shape[1:], BF16)
            flank_s[side] = jnp.full(flank_s.shape[1:], LOW, F32)

        @pl.when(jnp.logical_not(there & far))
        def _():
            ext[:, side * CORNER : (side + 1) * CORNER, :] = jnp.zeros(
                (2 * FRAMES, CORNER, HEADS * DIM), BF16
            )
    for t, (there, _) in enumerate(corners):
        @pl.when(jnp.logical_not(there))
        def _():
            rows = slice(t * CORNER, (t + 1) * CORNER)
            q_corner[rows, :] = jnp.zeros((CORNER, HEADS * DIM), BF16)
            corner_o[rows, :] = jnp.zeros((CORNER, HEADS * DIM), BF16)
            corner_s[t] = jnp.full(corner_s.shape[1:], LOW, F32)

    loads[0].wait()
    q_pack[...] = dot_nn(pick[...], q_all[...]).astype(BF16)

    def remote(src, dst, sems, index, device):
        return pltpu.make_async_remote_copy(
            src_ref=src,
            dst_ref=dst,
            send_sem=sems.at[(0, *index)],
            recv_sem=sems.at[(1, *index)],
            device_id=device,
            device_id_type=MESH,
        )

    width = HEADS * DIM // CHUNKS

    def copy_q_edge(side, c, device):
        part = pl.ds(c * width, width)
        return remote(
            q_pack.at[pl.ds((1 - side) * EDGE, EDGE), part],
            q_edge.at[side, :, part],
            q_edge_sem,
            (side, c),
            device,
        )

    def copy_q_flank(side, device):
        return remote(
            q_all.at[pl.ds((1 - side) * (TOKENS - FLANK), FLANK)],
            q_flank.at[side],
            q_flank_sem,
            (side,),
            device,
        )

    def corner_rows(t):
        return pl.ds(t // 2 * EDGE + t % 2 * (EDGE - CORNER), CORNER)

    def copy_q_corner(t, device):
        return remote(
            q_pack.at[corner_rows(t)],
            q_corner.at[pl.ds((CORNERS - 1 - t) * CORNER, CORNER)],
            q_corner_sem,
            (CORNERS - 1 - t,),
            device,
        )

    def copy_ext(side, device):
        start = (1 - side) * (EDGE - CORNER) + (1 - flip) * EDGE
        return remote(
            kv_pack.at[:, pl.ds(pl.multiple_of(start, CORNER), CORNER)],
            ext.at[:, pl.ds(side * CORNER, CORNER)],
            ext_sem,
            (side,),
            device,
        )

    def copy_edge_o(side, c, device):
        part = pl.ds(c * width, width)
        return remote(
            send_o.at[side, :, part],
            edge_o.at[1 - side, :, part],
            edge_sem,
            (1 - side, c),
            device,
        )

    def copy_edge_s(side, device):
        return remote(send_s.at[side], edge_s.at[1 - side], stat_sem, (1 - side,), device)

    def copy_flank_o(side, device):
        return remote(send_o.at[2 + side], flank_o.at[1 - side], flank_sem, (1 - side,), device)

    def copy_flank_s(side, device):
        return remote(send_s.at[2 + side], flank_s.at[1 - side], stat_sem, (3 - side,), device)

    def copy_corner_o(t, device):
        return remote(
            send_o.at[4, pl.ds(t * CORNER, CORNER)],
            corner_o.at[pl.ds((CORNERS - 1 - t) * CORNER, CORNER)],
            corner_sem,
            (CORNERS - 1 - t,),
            device,
        )

    def copy_corner_s(t, device):
        return remote(
            send_s.at[4], corner_s.at[CORNERS - 1 - t], stat_sem, (7 - t,), device
        )

    def to_via(src, dst, index):
        return remote(src, dst, via_sem, (index,), my_via)

    def onward(src, dst, index, there_sem):
        return pltpu.make_async_remote_copy(
            src_ref=src,
            dst_ref=dst,
            send_sem=onward_sem.at[index],
            recv_sem=there_sem,
            device_id=target,
            device_id_type=MESH,
        )

    def to_via_q(c):
        part = pl.ds(c * width, width)
        start = pl.multiple_of((1 - flip) * EDGE, EDGE)
        return to_via(q_pack.at[pl.ds(start, EDGE), part], via_q.at[:, part], c)

    def far_q(c):
        part = pl.ds(c * width, width)
        start = pl.multiple_of((1 - flip) * EDGE, EDGE)
        return remote(
            q_pack.at[pl.ds(start, EDGE), part],
            q_edge.at[flip, :, part],
            q_edge_sem,
            (flip, c),
            across,
        )

    def to_via_o(c):
        part = pl.ds(c * width, width)
        return to_via(send_o.at[1 - flip, :, part], via_o.at[:, part], CHUNKS + c)

    def to_via_s():
        return to_via(send_s.at[1 - flip], via_s, 2 * CHUNKS)

    def onward_q(c):
        part = pl.ds(c * width, width)
        return onward(
            via_q.at[:, part], q_edge.at[far_side, :, part], c, q_edge_sem.at[1, far_side, c]
        )

    def onward_o(c):
        part = pl.ds(c * width, width)
        return onward(
            via_o.at[:, part], edge_o.at[far_side, :, part], CHUNKS + c, edge_sem.at[1, far_side, c]
        )

    def onward_s():
        return onward(via_s, edge_s.at[far_side], 2 * CHUNKS, stat_sem.at[1, far_side])

    pl.semaphore_wait(barrier, sum(there.astype(jnp.int32) for there in awaited))

    for c in range(CHUNKS):
        @pl.when(far_via)
        def _():
            to_via_q(c).start()

        @pl.when(far_direct & jnp.logical_not(patient))
        def _():
            far_q(c).start()

        @pl.when(near_down)
        def _():
            copy_q_edge(0, c, down).start()

        @pl.when(near_up)
        def _():
            copy_q_edge(1, c, up).start()

    @pl.when(patient)
    def _():
        for c in range(CHUNKS):
            far_q(c).start()

    @pl.when(has_right)
    def _():
        copy_q_flank(0, right).start()

    @pl.when(has_left)
    def _():
        copy_q_flank(1, left).start()

    for t, (there, device) in enumerate(corners):
        @pl.when(there)
        def _():
            copy_q_corner(t, device).start()

    for slot in range(2 * FRAMES):
        loads[1 + slot].wait()
        kv_pack[slot] = dot_nn(pick[...], kv_all[slot]).astype(BF16)

    @pl.when(far & has_right)
    def _():
        copy_ext(0, right).start()

    @pl.when(far & has_left)
    def _():
        copy_ext(1, left).start()

    q, k = iota(bias0.shape, 0), iota(bias0.shape, 1)
    bias0[...] = mask((abs(q // ROWS - k // ROWS) <= RADIUS) & (abs(q % ROWS - k % ROWS) <= RADIUS))
    q, k = iota(bias1.shape, 0) + REACH1, iota(bias1.shape, 1) + BLOCK1
    bias1[...] = mask(
        (abs(q // ROWS - k // ROWS) <= RADIUS) & (abs(q % ROWS - k % ROWS) <= RADIUS) & (k >= CUT)
    )

    q, k = iota(bias_flank.shape[1:], 0), iota(bias_flank.shape[1:], 1)
    rows_near = (abs(q % ROWS - k % ROWS) <= RADIUS) & (k < FRAMES * FLANK)
    k = k % FLANK
    bias_flank[0] = mask(rows_near & (k // ROWS <= q // ROWS))
    bias_flank[1] = mask(rows_near & (k // ROWS >= q // ROWS))

    def real_slot(slot):
        return (slot < COLS - RADIUS) | (slot >= SLOTS - RADIUS)

    q, k = iota(bias_near.shape[1:], 0), iota(bias_near.shape[1:], 1)
    slot = k % EDGE // RADIUS
    cols_near = abs(edge_col(q // RADIUS) - edge_col(slot)) <= RADIUS
    cols_near = cols_near & real_slot(slot) & (k < FRAMES * EDGE)
    bias_near[0] = mask(cols_near & (k % RADIUS <= q % RADIUS))
    bias_near[1] = mask(cols_near & (k % RADIUS >= q % RADIUS))

    q, k = iota(bias_far.shape, 0), iota(bias_far.shape, 1) % SPAN
    slot = k // RADIUS
    in_left = (k >= EDGE) & (k < EDGE + CORNER)
    in_right = k >= EDGE + CORNER
    key_col = jnp.where(
        in_left, slot - SLOTS - RADIUS, jnp.where(in_right, slot - SLOTS - RADIUS + COLS, edge_col(slot))
    )
    real = jnp.where(
        in_left,
        (far & has_left).astype(jnp.int32),
        jnp.where(in_right, (far & has_right).astype(jnp.int32), real_slot(slot).astype(jnp.int32)),
    )
    sign = 2 * flip - 1
    rows_near = (q % RADIUS - k % RADIUS) * sign >= 0
    bias_far[...] = mask((abs(edge_col(q // RADIUS) - key_col) <= RADIUS) & (real > 0) & rows_near)

    q, k = iota(bias_corner.shape, 0), iota(bias_corner.shape, 1)
    same = (q // CORNER == k % EDGE // CORNER) & (k < FRAMES * EDGE)
    down_sign, right_sign = 1 - q // CORNER // 2 * 2, 1 - q // CORNER % 2 * 2
    rows_near = (q % RADIUS - k % RADIUS) * down_sign >= 0
    cols_near = (q % CORNER // RADIUS - k % CORNER // RADIUS) * right_sign >= 0
    bias_corner[...] = mask(same & rows_near & cols_near)

    def own_head(head):
        at = lanes(head)

        def block(kv, first, size):
            return jnp.concatenate(
                [kv_all[kv * FRAMES + f, pl.ds(first, size), at] for f in range(FRAMES)], axis=0
            )

        s0 = dot_nt(q_all[0:REACH0, at], block(0, 0, CUT)) + jnp.concatenate(
            [bias0[...]] * FRAMES, axis=1
        )
        s1 = dot_nt(q_all[REACH1:TOKENS, at], block(0, BLOCK1, CUT)) + jnp.concatenate(
            [bias1[...]] * FRAMES, axis=1
        )
        t0 = jnp.max(s0, axis=1, keepdims=True)
        t1 = jnp.max(s1, axis=1, keepdims=True)
        both = REACH0 - REACH1
        top = FOLD * jnp.concatenate(
            [t0[0:REACH1], jnp.maximum(t0[REACH1:], t1[0:both]), t1[both:]], axis=0
        )
        top = top.astype(BF16).astype(F32)
        o0 = dot_nn(soft(s0, top[0:REACH0]), with_ones(block(1, 0, CUT)))
        o1 = dot_nn(soft(s1, top[REACH1:TOKENS]), with_ones(block(1, BLOCK1, CUT)))
        o = jnp.concatenate([o0[0:REACH1], o0[REACH1:] + o1[0:both], o1[both:]], axis=0)
        own_o[head] = o[:, :DIM]
        own_l[head] = o[:, DIM:]
        own_m[head] = jnp.broadcast_to(top, (TOKENS, DIM))

    def own_heads(i, carry):
        for j in range(OWN_UNROLL):
            own_head(i * OWN_UNROLL + j)
        return carry

    lax.fori_loop(0, HEADS // OWN_UNROLL, own_heads, 0)

    lane = iota((GROUP, DIM), 1)

    def guest(head, stat, q, k, v, bias):
        s = dot_nt(q, k) + bias
        top = offset(s)
        o = dot_nn(soft(s, top), with_ones(v))
        for t in range(4):
            rows = slice(t * GROUP, (t + 1) * GROUP)
            stat = jnp.where(lane == 32 * t + head, top[rows], stat)
            stat = jnp.where(lane == 32 * t + HEADS + head, o[rows, DIM:], stat)
        return o[:, :DIM].astype(BF16), stat

    sides = ((0, has_left, left), (1, has_right, right))
    for side, there, device in sides:
        @pl.when(there)
        def _():
            copy_q_flank(side, device).wait_recv()

    stats = [jnp.zeros((GROUP, DIM), F32)] * 2
    for head in range(HEADS):
        at = lanes(head)
        for side in range(2):
            part = pl.ds(side * (TOKENS - FLANK), FLANK)
            k = jnp.concatenate([kv_all[f, part, at] for f in (0, 1, 2, 0)], axis=0)
            v = jnp.concatenate([kv_all[FRAMES + f, part, at] for f in (0, 1, 2, 0)], axis=0)
            o, stats[side] = guest(head, stats[side], q_flank[side, :, at], k, v, bias_flank[side])
            send_o[2 + side, :, at] = o
    for side, there, device in sides:
        send_s[2 + side] = stats[side]

        @pl.when(there)
        def _():
            copy_flank_o(side, device).start()
            copy_flank_s(side, device).start()

    def near_head(side, head, stat):
        at = lanes(head)
        part = pl.ds(pl.multiple_of(side * EDGE, EDGE), EDGE)
        k = jnp.concatenate([kv_pack[f, part, at] for f in (0, 1, 2, 0)], axis=0)
        v = jnp.concatenate([kv_pack[FRAMES + f, part, at] for f in (0, 1, 2, 0)], axis=0)
        o, stat = guest(head, stat, q_edge[side, :, at], k, v, bias_near[side])
        send_o[side, :, at] = o
        return stat

    def far_head(side, head, stat):
        at = lanes(head)
        part = pl.ds(pl.multiple_of(side * EDGE, EDGE), EDGE)

        def keys(kv):
            pieces = []
            for f in range(FRAMES):
                pieces.append(kv_pack[kv * FRAMES + f, part, at])
                pieces.append(ext[kv * FRAMES + f, :, at])
            return jnp.concatenate(pieces, axis=0)

        o, stat = guest(head, stat, q_edge[side, :, at], keys(0), keys(1), bias_far[...])
        send_o[side, :, at] = o
        return stat

    def edge_of(turn):
        side = (turn + flip) % 2
        there = jnp.where(side == 0, has_up.astype(jnp.int32), has_down.astype(jnp.int32)) > 0
        return side, there, (h - 1 + 2 * side, w)

    per = HEADS // CHUNKS
    side, there, device = edge_of(0)

    @pl.when(there)
    def _():
        for c in range(CHUNKS):
            copy_q_edge(side, c, device).wait_recv()
        stat = jnp.zeros((GROUP, DIM), F32)
        for head in range(HEADS):
            stat = near_head(side, head, stat)
        send_s[side] = stat
        for c in range(CHUNKS):
            copy_edge_o(side, c, device).start()
        copy_edge_s(side, device).start()

    for t, (there, device) in enumerate(corners):
        @pl.when(there)
        def _():
            copy_q_corner(CORNERS - 1 - t, device).wait_recv()

    stat = jnp.zeros((GROUP, DIM), F32)
    for head in range(HEADS):
        at = lanes(head)

        def corner_keys(kv):
            pieces = []
            for f in (0, 1, 2, 0):
                for t in range(CORNERS):
                    pieces.append(kv_pack[kv * FRAMES + f, corner_rows(t), at])
            return jnp.concatenate(pieces, axis=0)

        o, stat = guest(
            head, stat, q_corner[:, at], corner_keys(0), corner_keys(1), bias_corner[...]
        )
        send_o[4, :, at] = o
    send_s[4] = stat
    for t, (there, device) in enumerate(corners):
        @pl.when(there)
        def _():
            copy_corner_o(t, device).start()
            copy_corner_s(t, device).start()

    for side, there, device in sides:
        @pl.when(there & far)
        def _():
            copy_ext(side, device).wait_recv()

    side1, there1, device1 = edge_of(1)

    @pl.when(there1)
    def _():
        stat = jnp.zeros((GROUP, DIM), F32)
        for c in range(CHUNKS):
            copy_q_edge(side1, c, device1).wait_recv()
            for i in range(per):
                stat = far_head(side1, c * per + i, stat)

            @pl.when(far_via)
            def _():
                to_via_o(c).start()

            @pl.when(jnp.logical_not(far_via))
            def _():
                copy_edge_o(side1, c, device1).start()

        send_s[side1] = stat

        @pl.when(far_via)
        def _():
            to_via_s().start()

        @pl.when(jnp.logical_not(far_via))
        def _():
            copy_edge_s(side1, device1).start()

    @pl.when(serves)
    def _():
        for c in range(CHUNKS):
            to_via_q(c).wait_recv()
            onward_q(c).start()

    for side, there, device in sides:
        @pl.when(there)
        def _():
            copy_flank_o(1 - side, device).wait_recv()
            copy_flank_s(1 - side, device).wait_recv()

    def column(stat, index):
        return jnp.concatenate(
            [stat[:, 32 * t + index : 32 * t + index + 1] for t in range(4)], axis=0
        )

    def merge(own, other):
        (m0, l0, o0), (m1, l1, o1) = own, other
        top = jnp.maximum(m0, m1)
        a0, a1 = jnp.exp2(m0 - top), jnp.exp2(m1 - top)
        return top, a0 * l0 + a1 * jnp.maximum(l1, 0.0), a0 * o0 + a1 * o1.astype(F32)

    wide_lane = iota((TOKENS, DIM), 1)
    own_stat = jnp.zeros((TOKENS, DIM), F32)
    for head in range(HEADS):
        at = lanes(head)
        for side in range(2):
            part = pl.ds(side * (TOKENS - FLANK), FLANK)
            stat = flank_s[side]
            top, total, mixed = merge(
                (own_m[head, part], own_l[head, part], own_o[head, part]),
                (column(stat, head), column(stat, HEADS + head), flank_o[side, :, at]),
            )
            own_m[head, part] = top
            own_l[head, part] = total
            own_o[head, part] = mixed
        total = own_l[head]
        high = total.astype(BF16).astype(F32)
        own_stat = jnp.where(wide_lane == head, own_m[head], own_stat)
        own_stat = jnp.where(wide_lane == HEADS + head, high, own_stat)
        own_stat = jnp.where(wide_lane == 2 * HEADS + head, total - high, own_stat)
    packed_stat = dot_nn(pick[...], own_stat.astype(BF16))
    inner = iota((TOKENS, DIM), 0) % ROWS
    inner = (inner >= RADIUS) & (inner < ROWS - RADIUS)
    for head in range(HEADS):
        at = lanes(head)
        o = own_o[head]
        high = o.astype(BF16)
        rest = (o - high.astype(F32)).astype(BF16)
        edge_own_o[head] = dot_nn(pick[...], high) + dot_nn(pick[...], rest)
        edge_own_m[head] = jnp.broadcast_to(packed_stat[:, head : head + 1], (2 * EDGE, DIM))
        edge_own_l[head] = jnp.broadcast_to(
            packed_stat[:, HEADS + head : HEADS + head + 1]
            + packed_stat[:, 2 * HEADS + head : 2 * HEADS + head + 1],
            (2 * EDGE, DIM),
        )
        out[:, at] = jnp.where(inner, o / own_l[head], 0.0).astype(BF16)

    for t, (there, device) in enumerate(corners):
        @pl.when(there)
        def _():
            copy_corner_o(CORNERS - 1 - t, device).wait_recv()
            copy_corner_s(CORNERS - 1 - t, device).wait_recv()

    slot = iota((EDGE, DIM), 0) // RADIUS
    real = real_slot(slot)
    for side in range(2):
        for lr in range(2):
            t = 2 * side + lr
            part = pl.ds(side * EDGE + lr * (EDGE - CORNER), CORNER)
            first = 32 * (CORNERS - 1 - t)
            stat = corner_s[t]
            for head in range(HEADS):
                m1 = stat[:, first + head : first + head + 1]
                l1 = stat[:, first + HEADS + head : first + HEADS + head + 1]
                o1 = corner_o[t * CORNER : (t + 1) * CORNER, lanes(head)]
                top, total, mixed = merge(
                    (edge_own_m[head, part], edge_own_l[head, part], edge_own_o[head, part]),
                    (m1, l1, o1),
                )
                edge_own_m[head, part] = top
                edge_own_l[head, part] = total
                edge_own_o[head, part] = mixed

    for turn in range(2):
        side, there, device = edge_of(turn)
        part = pl.ds(pl.multiple_of(side * EDGE, EDGE), EDGE)
        place = jnp.where(side == 0, spread[:, 0:EDGE], spread[:, EDGE : 2 * EDGE])

        @pl.when(there)
        def _():
            for c in range(CHUNKS):
                copy_edge_o(1 - side, c, device).wait_recv()
            copy_edge_s(1 - side, device).wait_recv()

        stat = edge_s[side]
        for head in range(HEADS):
            at = lanes(head)
            top, total, mixed = merge(
                (edge_own_m[head, part], edge_own_l[head, part], edge_own_o[head, part]),
                (column(stat, head), column(stat, HEADS + head), edge_o[side, :, at]),
            )
            done = jnp.where(real, mixed / total, 0.0).astype(BF16)
            out[:, at] = out[:, at] + dot_nn(place, done).astype(BF16)

    @pl.when(serves)
    def _():
        for c in range(CHUNKS):
            to_via_o(c).wait_recv()
            onward_o(c).start()
        to_via_s().wait_recv()
        onward_s().start()
        for c in range(CHUNKS):
            onward_q(c).wait_send()
            onward_o(c).wait_send()
        onward_s().wait_send()

    @pl.when(far_via)
    def _():
        for c in range(CHUNKS):
            to_via_q(c).wait_send()
            to_via_o(c).wait_send()
        to_via_s().wait_send()

    @pl.when(far_direct)
    def _():
        for c in range(CHUNKS):
            far_q(c).wait_send()
            copy_edge_o(side1, c, device1).wait_send()
        copy_edge_s(side1, device1).wait_send()

    for c in range(CHUNKS):
        @pl.when(near_down)
        def _():
            copy_q_edge(0, c, down).wait_send()
            copy_edge_o(1, c, down).wait_send()

        @pl.when(near_up)
        def _():
            copy_q_edge(1, c, up).wait_send()
            copy_edge_o(0, c, up).wait_send()

    @pl.when(near_down)
    def _():
        copy_edge_s(1, down).wait_send()

    @pl.when(near_up)
    def _():
        copy_edge_s(0, up).wait_send()

    for side, there, device in ((0, has_right, right), (1, has_left, left)):
        @pl.when(there)
        def _():
            copy_q_flank(side, device).wait_send()
            copy_flank_o(1 - side, device).wait_send()
            copy_flank_s(1 - side, device).wait_send()

        @pl.when(there & far)
        def _():
            copy_ext(side, device).wait_send()

    for t, (there, device) in enumerate(corners):
        @pl.when(there)
        def _():
            copy_q_corner(t, device).wait_send()
            copy_corner_o(t, device).wait_send()
            copy_corner_s(t, device).wait_send()


def on_device(nh, nw, queries, kv_new, kv_past):
    wide = HEADS * DIM
    hbm = pl.BlockSpec(memory_space=pltpu.HBM)
    dma = pltpu.SemaphoreType.DMA
    queries = queries.transpose(1, 0, 2).reshape(TOKENS, wide)
    kv_new = kv_new.transpose(0, 2, 1, 3).reshape(2, TOKENS, wide)
    kv_past = kv_past.transpose(0, 1, 3, 2, 4).reshape(FRAMES - 1, 2, TOKENS, wide)
    out = pl.pallas_call(
        functools.partial(kernel, nh, nw),
        out_shape=jax.ShapeDtypeStruct((TOKENS, wide), BF16),
        in_specs=[hbm] * 3,
        out_specs=pl.BlockSpec(memory_space=pltpu.VMEM),
        scratch_shapes=[
            pltpu.VMEM((TOKENS, wide), BF16),
            pltpu.VMEM((2 * FRAMES, TOKENS, wide), BF16),
            pltpu.VMEM((2 * EDGE, wide), BF16),
            pltpu.VMEM((2 * FRAMES, 2 * EDGE, wide), BF16),
            pltpu.VMEM((2, EDGE, wide), BF16),
            pltpu.VMEM((2, FLANK, wide), BF16),
            pltpu.VMEM((CORNERS * CORNER, wide), BF16),
            pltpu.VMEM((2 * FRAMES, 2 * CORNER, wide), BF16),
            pltpu.VMEM((HEADS, TOKENS, DIM), F32),
            pltpu.VMEM((HEADS, TOKENS, DIM), F32),
            pltpu.VMEM((HEADS, TOKENS, DIM), F32),
            pltpu.VMEM((HEADS, 2 * EDGE, DIM), F32),
            pltpu.VMEM((HEADS, 2 * EDGE, DIM), F32),
            pltpu.VMEM((HEADS, 2 * EDGE, DIM), F32),
            pltpu.VMEM((5, EDGE, wide), BF16),
            pltpu.VMEM((5, GROUP, DIM), F32),
            pltpu.VMEM((2, EDGE, wide), BF16),
            pltpu.VMEM((2, GROUP, DIM), F32),
            pltpu.VMEM((2, FLANK, wide), BF16),
            pltpu.VMEM((2, GROUP, DIM), F32),
            pltpu.VMEM((CORNERS * CORNER, wide), BF16),
            pltpu.VMEM((CORNERS, GROUP, DIM), F32),
            pltpu.VMEM((EDGE, wide), BF16),
            pltpu.VMEM((EDGE, wide), BF16),
            pltpu.VMEM((GROUP, DIM), F32),
            pltpu.VMEM((REACH0, CUT), F32),
            pltpu.VMEM((TOKENS - REACH1, CUT), F32),
            pltpu.VMEM((2, FLANK, (FRAMES + 1) * FLANK), F32),
            pltpu.VMEM((2, EDGE, (FRAMES + 1) * EDGE), F32),
            pltpu.VMEM((EDGE, FRAMES * SPAN), F32),
            pltpu.VMEM((EDGE, (FRAMES + 1) * EDGE), F32),
            pltpu.VMEM((2 * EDGE, TOKENS), BF16),
            pltpu.VMEM((TOKENS, 2 * EDGE), BF16),
            dma((1 + 2 * FRAMES,)),
            dma((2, 2, CHUNKS)),
            dma((2, 2)),
            dma((2, CORNERS)),
            dma((2, 2)),
            dma((2, 2, CHUNKS)),
            dma((2, 2)),
            dma((2, CORNERS)),
            dma((2, 8)),
            dma((2, 2 * CHUNKS + 1)),
            dma((2 * CHUNKS + 1,)),
        ],
        compiler_params=pltpu.CompilerParams(
            collective_id=0, has_side_effects=True, vmem_limit_bytes=VMEM_BYTES
        ),
    )(queries, kv_new, kv_past)
    return out.reshape(COLS, ROWS, wide).transpose(1, 0, 2)


def solution(mesh):
    return jax.shard_map(
        functools.partial(on_device, mesh.shape["ha"], mesh.shape["wa"]),
        mesh=mesh,
        in_specs=(P("ha", "wa", None), P(None, "ha", "wa", None), P(None, None, "ha", "wa", None)),
        out_specs=P("ha", "wa", None),
        check_vma=False,
    )
```

```python
import functools
import math

import jax
import jax.numpy as jnp
from jax import lax
from jax.experimental import pallas as pl
from jax.experimental.pallas import tpu as pltpu
from jax.sharding import PartitionSpec as P

MESH = pl.DeviceIdType.MESH
HEADS = 8
DIM = 128
RADIUS = 4
FRAMES = 3
ROWS = 16
COLS = 14
TOKENS = ROWS * COLS
FLANK = RADIUS * ROWS
SLOTS = 16
EDGE = SLOTS * RADIUS
CORNER = RADIUS * RADIUS
SPAN = EDGE + 2 * CORNER
CORNERS = 4
GROUP = 16
CHUNKS = 2
LOW = -1e30
VMEM_BYTES = 54579 * 1024
FOLD = math.log2(math.e) / math.sqrt(DIM)
F32 = jnp.float32
BF16 = jnp.bfloat16
CUT = 8 * ROWS
BLOCK1 = TOKENS - CUT
REACH0 = 12 * ROWS
REACH1 = 4 * ROWS
OWN_UNROLL = 8


def dot_nt(a, b):
    return lax.dot_general(a, b, (((1,), (1,)), ((), ())), preferred_element_type=F32)


def dot_nn(a, b):
    return lax.dot_general(a, b, (((1,), (0,)), ((), ())), preferred_element_type=F32)


def iota(shape, dim):
    return lax.broadcasted_iota(jnp.int32, shape, dim)


def lanes(head):
    if isinstance(head, int):
        return pl.ds(head * DIM, DIM)
    return pl.ds(pl.multiple_of(head * DIM, DIM), DIM)


def mask(allowed):
    return jnp.where(allowed, 0.0, LOW)


def edge_col(slot):
    return jnp.where(slot < COLS - RADIUS, slot, slot - (SLOTS - COLS))


def soft(scores, top):
    return jnp.exp2(scores * FOLD - top).astype(BF16)


def with_ones(values):
    return jnp.concatenate([values, jnp.ones_like(values)], axis=1)


def offset(scores):
    top = FOLD * jnp.max(scores, axis=1, keepdims=True)
    return top.astype(BF16).astype(F32)


def kernel(
    nh, nw,
    q_hbm, new_hbm, past_hbm, out,
    q_all, kv_all, q_pack, kv_pack,
    q_edge, q_flank, q_corner, ext, own_o, own_m, own_l, edge_own_o, edge_own_m, edge_own_l,
    send_o, send_s, edge_o, edge_s, flank_o, flank_s, corner_o, corner_s,
    via_q, via_o, via_s,
    bias0, bias1, bias_flank, bias_near, bias_far, bias_corner, pick, spread,
    load_sem, q_edge_sem, q_flank_sem, q_corner_sem, ext_sem,
    edge_sem, flank_sem, corner_sem, stat_sem, via_sem, onward_sem,
):
    h = lax.axis_index("ha")
    w = lax.axis_index("wa")
    has_up, has_down = h > 0, h < nh - 1
    has_left, has_right = w > 0, w < nw - 1
    up, down = (h - 1, w), (h + 1, w)
    left, right = (h, w - 1), (h, w + 1)
    flip = (h == nh // 2).astype(jnp.int32)
    far_up, far_down = h == nh // 2, h == nh // 2 - 1
    far = far_up | far_down
    near_up, near_down = has_up & (h != nh // 2), has_down & (h != nh // 2 - 1)
    corners = (
        (near_up & has_left, (h - 1, w - 1)),
        (near_up & has_right, (h - 1, w + 1)),
        (near_down & has_left, (h + 1, w - 1)),
        (near_down & has_right, (h + 1, w + 1)),
    )
    near = ((near_up, up), (near_down, down), (has_left, left), (has_right, right)) + corners

    relayed = (w >= nw // 2) & ((w // 4 - nw // 8) % 2 == 1)
    via_down, via_up = nh // 2 + 2, nh // 2 - 3
    serves_down, serves_up = relayed & (h == via_down), relayed & (h == via_up)
    serves = serves_down | serves_up
    far_side = serves_up.astype(jnp.int32)
    served, target = (nh // 2 - 1 + far_side, w), (nh // 2 - far_side, w)
    my_via = (jnp.where(far_down, via_down, via_up), w)
    other_via = (jnp.where(far_down, via_up, via_down), w)
    far_via, far_direct = far & relayed, far & jnp.logical_not(relayed)
    across = (nh // 2 - flip, w)
    patient = far_down & far_direct & (w // 4 == nw // 8 - 1)
    greet = near + ((far_via, other_via), (far_direct, across), (serves, served))
    awaited = [there for there, _ in near] + [far, serves]

    barrier = pltpu.get_barrier_semaphore()
    for there, device in greet:
        @pl.when(there)
        def _():
            pl.semaphore_signal(barrier, inc=1, device_id=device, device_id_type=MESH)

    loads = [pltpu.make_async_copy(q_hbm, q_all, load_sem.at[0])]
    for kv in range(2):
        for f in range(FRAMES):
            source = new_hbm.at[kv] if f == FRAMES - 1 else past_hbm.at[f, kv]
            slot = kv * FRAMES + f
            loads.append(pltpu.make_async_copy(source, kv_all.at[slot], load_sem.at[1 + slot]))
    for load in loads:
        load.start()

    def picked(shape, dim):
        i, t = iota(shape, dim), iota(shape, 1 - dim)
        slot = i % EDGE // RADIUS
        real = (slot < COLS - RADIUS) | (slot >= SLOTS - RADIUS)
        token = edge_col(slot) * ROWS + i % RADIUS + i // EDGE * (ROWS - RADIUS)
        return jnp.where(real & (t == token), 1.0, 0.0).astype(BF16)

    pick[...] = picked((2 * EDGE, TOKENS), 0)
    spread[...] = picked((TOKENS, 2 * EDGE), 1)

    for there, side in ((has_up, 0), (has_down, 1)):
        @pl.when(jnp.logical_not(there))
        def _():
            q_edge[side] = jnp.zeros(q_edge.shape[1:], BF16)
            edge_o[side] = jnp.zeros(edge_o.shape[1:], BF16)
            edge_s[side] = jnp.full(edge_s.shape[1:], LOW, F32)
    for there, side in ((has_left, 0), (has_right, 1)):
        @pl.when(jnp.logical_not(there))
        def _():
            q_flank[side] = jnp.zeros(q_flank.shape[1:], BF16)
            flank_o[side] = jnp.zeros(flank_o.shape[1:], BF16)
            flank_s[side] = jnp.full(flank_s.shape[1:], LOW, F32)

        @pl.when(jnp.logical_not(there & far))
        def _():
            ext[:, side * CORNER : (side + 1) * CORNER, :] = jnp.zeros(
                (2 * FRAMES, CORNER, HEADS * DIM), BF16
            )
    for t, (there, _) in enumerate(corners):
        @pl.when(jnp.logical_not(there))
        def _():
            rows = slice(t * CORNER, (t + 1) * CORNER)
            q_corner[rows, :] = jnp.zeros((CORNER, HEADS * DIM), BF16)
            corner_o[rows, :] = jnp.zeros((CORNER, HEADS * DIM), BF16)
            corner_s[t] = jnp.full(corner_s.shape[1:], LOW, F32)

    loads[0].wait()
    q_pack[...] = dot_nn(pick[...], q_all[...]).astype(BF16)

    def remote(src, dst, sems, index, device):
        return pltpu.make_async_remote_copy(
            src_ref=src,
            dst_ref=dst,
            send_sem=sems.at[(0, *index)],
            recv_sem=sems.at[(1, *index)],
            device_id=device,
            device_id_type=MESH,
        )

    width = HEADS * DIM // CHUNKS

    def copy_q_edge(side, c, device):
        part = pl.ds(c * width, width)
        return remote(
            q_pack.at[pl.ds((1 - side) * EDGE, EDGE), part],
            q_edge.at[side, :, part],
            q_edge_sem,
            (side, c),
            device,
        )

    def copy_q_flank(side, device):
        return remote(
            q_all.at[pl.ds((1 - side) * (TOKENS - FLANK), FLANK)],
            q_flank.at[side],
            q_flank_sem,
            (side,),
            device,
        )

    def corner_rows(t):
        return pl.ds(t // 2 * EDGE + t % 2 * (EDGE - CORNER), CORNER)

    def copy_q_corner(t, device):
        return remote(
            q_pack.at[corner_rows(t)],
            q_corner.at[pl.ds((CORNERS - 1 - t) * CORNER, CORNER)],
            q_corner_sem,
            (CORNERS - 1 - t,),
            device,
        )

    def copy_ext(side, device):
        start = (1 - side) * (EDGE - CORNER) + (1 - flip) * EDGE
        return remote(
            kv_pack.at[:, pl.ds(pl.multiple_of(start, CORNER), CORNER)],
            ext.at[:, pl.ds(side * CORNER, CORNER)],
            ext_sem,
            (side,),
            device,
        )

    def copy_edge_o(side, c, device):
        part = pl.ds(c * width, width)
        return remote(
            send_o.at[side, :, part],
            edge_o.at[1 - side, :, part],
            edge_sem,
            (1 - side, c),
            device,
        )

    def copy_edge_s(side, device):
        return remote(send_s.at[side], edge_s.at[1 - side], stat_sem, (1 - side,), device)

    def copy_flank_o(side, device):
        return remote(send_o.at[2 + side], flank_o.at[1 - side], flank_sem, (1 - side,), device)

    def copy_flank_s(side, device):
        return remote(send_s.at[2 + side], flank_s.at[1 - side], stat_sem, (3 - side,), device)

    def copy_corner_o(t, device):
        return remote(
            send_o.at[4, pl.ds(t * CORNER, CORNER)],
            corner_o.at[pl.ds((CORNERS - 1 - t) * CORNER, CORNER)],
            corner_sem,
            (CORNERS - 1 - t,),
            device,
        )

    def copy_corner_s(t, device):
        return remote(
            send_s.at[4], corner_s.at[CORNERS - 1 - t], stat_sem, (7 - t,), device
        )

    def to_via(src, dst, index):
        return remote(src, dst, via_sem, (index,), my_via)

    def onward(src, dst, index, there_sem):
        return pltpu.make_async_remote_copy(
            src_ref=src,
            dst_ref=dst,
            send_sem=onward_sem.at[index],
            recv_sem=there_sem,
            device_id=target,
            device_id_type=MESH,
        )

    def to_via_q(c):
        part = pl.ds(c * width, width)
        start = pl.multiple_of((1 - flip) * EDGE, EDGE)
        return to_via(q_pack.at[pl.ds(start, EDGE), part], via_q.at[:, part], c)

    def far_q(c):
        part = pl.ds(c * width, width)
        start = pl.multiple_of((1 - flip) * EDGE, EDGE)
        return remote(
            q_pack.at[pl.ds(start, EDGE), part],
            q_edge.at[flip, :, part],
            q_edge_sem,
            (flip, c),
            across,
        )

    def to_via_o(c):
        part = pl.ds(c * width, width)
        return to_via(send_o.at[1 - flip, :, part], via_o.at[:, part], CHUNKS + c)

    def to_via_s():
        return to_via(send_s.at[1 - flip], via_s, 2 * CHUNKS)

    def onward_q(c):
        part = pl.ds(c * width, width)
        return onward(
            via_q.at[:, part], q_edge.at[far_side, :, part], c, q_edge_sem.at[1, far_side, c]
        )

    def onward_o(c):
        part = pl.ds(c * width, width)
        return onward(
            via_o.at[:, part], edge_o.at[far_side, :, part], CHUNKS + c, edge_sem.at[1, far_side, c]
        )

    def onward_s():
        return onward(via_s, edge_s.at[far_side], 2 * CHUNKS, stat_sem.at[1, far_side])

    pl.semaphore_wait(barrier, sum(there.astype(jnp.int32) for there in awaited))

    for c in range(CHUNKS):
        @pl.when(far_via)
        def _():
            to_via_q(c).start()

        @pl.when(far_direct & jnp.logical_not(patient))
        def _():
            far_q(c).start()

        @pl.when(near_down)
        def _():
            copy_q_edge(0, c, down).start()

        @pl.when(near_up)
        def _():
            copy_q_edge(1, c, up).start()

    @pl.when(patient)
    def _():
        for c in range(CHUNKS):
            far_q(c).start()

    @pl.when(has_right)
    def _():
        copy_q_flank(0, right).start()

    @pl.when(has_left)
    def _():
        copy_q_flank(1, left).start()

    for t, (there, device) in enumerate(corners):
        @pl.when(there)
        def _():
            copy_q_corner(t, device).start()

    for slot in range(2 * FRAMES):
        loads[1 + slot].wait()
        kv_pack[slot] = dot_nn(pick[...], kv_all[slot]).astype(BF16)

    @pl.when(far & has_right)
    def _():
        copy_ext(0, right).start()

    @pl.when(far & has_left)
    def _():
        copy_ext(1, left).start()

    q, k = iota(bias0.shape, 0), iota(bias0.shape, 1)
    bias0[...] = mask((abs(q // ROWS - k // ROWS) <= RADIUS) & (abs(q % ROWS - k % ROWS) <= RADIUS))
    q, k = iota(bias1.shape, 0) + REACH1, iota(bias1.shape, 1) + BLOCK1
    bias1[...] = mask(
        (abs(q // ROWS - k // ROWS) <= RADIUS) & (abs(q % ROWS - k % ROWS) <= RADIUS) & (k >= CUT)
    )

    q, k = iota(bias_flank.shape[1:], 0), iota(bias_flank.shape[1:], 1)
    rows_near = (abs(q % ROWS - k % ROWS) <= RADIUS) & (k < FRAMES * FLANK)
    k = k % FLANK
    bias_flank[0] = mask(rows_near & (k // ROWS <= q // ROWS))
    bias_flank[1] = mask(rows_near & (k // ROWS >= q // ROWS))

    def real_slot(slot):
        return (slot < COLS - RADIUS) | (slot >= SLOTS - RADIUS)

    q, k = iota(bias_near.shape[1:], 0), iota(bias_near.shape[1:], 1)
    slot = k % EDGE // RADIUS
    cols_near = abs(edge_col(q // RADIUS) - edge_col(slot)) <= RADIUS
    cols_near = cols_near & real_slot(slot) & (k < FRAMES * EDGE)
    bias_near[0] = mask(cols_near & (k % RADIUS <= q % RADIUS))
    bias_near[1] = mask(cols_near & (k % RADIUS >= q % RADIUS))

    q, k = iota(bias_far.shape, 0), iota(bias_far.shape, 1) % SPAN
    slot = k // RADIUS
    in_left = (k >= EDGE) & (k < EDGE + CORNER)
    in_right = k >= EDGE + CORNER
    key_col = jnp.where(
        in_left, slot - SLOTS - RADIUS, jnp.where(in_right, slot - SLOTS - RADIUS + COLS, edge_col(slot))
    )
    real = jnp.where(
        in_left,
        (far & has_left).astype(jnp.int32),
        jnp.where(in_right, (far & has_right).astype(jnp.int32), real_slot(slot).astype(jnp.int32)),
    )
    sign = 2 * flip - 1
    rows_near = (q % RADIUS - k % RADIUS) * sign >= 0
    bias_far[...] = mask((abs(edge_col(q // RADIUS) - key_col) <= RADIUS) & (real > 0) & rows_near)

    q, k = iota(bias_corner.shape, 0), iota(bias_corner.shape, 1)
    same = (q // CORNER == k % EDGE // CORNER) & (k < FRAMES * EDGE)
    down_sign, right_sign = 1 - q // CORNER // 2 * 2, 1 - q // CORNER % 2 * 2
    rows_near = (q % RADIUS - k % RADIUS) * down_sign >= 0
    cols_near = (q % CORNER // RADIUS - k % CORNER // RADIUS) * right_sign >= 0
    bias_corner[...] = mask(same & rows_near & cols_near)

    def own_head(head):
        at = lanes(head)

        def block(kv, first, size):
            return jnp.concatenate(
                [kv_all[kv * FRAMES + f, pl.ds(first, size), at] for f in range(FRAMES)], axis=0
            )

        s0 = dot_nt(q_all[0:REACH0, at], block(0, 0, CUT)) + jnp.concatenate(
            [bias0[...]] * FRAMES, axis=1
        )
        s1 = dot_nt(q_all[REACH1:TOKENS, at], block(0, BLOCK1, CUT)) + jnp.concatenate(
            [bias1[...]] * FRAMES, axis=1
        )
        t0 = jnp.max(s0, axis=1, keepdims=True)
        t1 = jnp.max(s1, axis=1, keepdims=True)
        both = REACH0 - REACH1
        top = FOLD * jnp.concatenate(
            [t0[0:REACH1], jnp.maximum(t0[REACH1:], t1[0:both]), t1[both:]], axis=0
        )
        top = top.astype(BF16).astype(F32)
        o0 = dot_nn(soft(s0, top[0:REACH0]), with_ones(block(1, 0, CUT)))
        o1 = dot_nn(soft(s1, top[REACH1:TOKENS]), with_ones(block(1, BLOCK1, CUT)))
        o = jnp.concatenate([o0[0:REACH1], o0[REACH1:] + o1[0:both], o1[both:]], axis=0)
        own_o[head] = o[:, :DIM]
        own_l[head] = o[:, DIM:]
        own_m[head] = jnp.broadcast_to(top, (TOKENS, DIM))

    def own_heads(i, carry):
        for j in range(OWN_UNROLL):
            own_head(i * OWN_UNROLL + j)
        return carry

    lax.fori_loop(0, HEADS // OWN_UNROLL, own_heads, 0)

    lane = iota((GROUP, DIM), 1)

    def guest(head, stat, q, k, v, bias):
        s = dot_nt(q, k) + bias
        top = offset(s)
        o = dot_nn(soft(s, top), with_ones(v))
        for t in range(4):
            rows = slice(t * GROUP, (t + 1) * GROUP)
            stat = jnp.where(lane == 32 * t + head, top[rows], stat)
            stat = jnp.where(lane == 32 * t + HEADS + head, o[rows, DIM:], stat)
        return o[:, :DIM].astype(BF16), stat

    sides = ((0, has_left, left), (1, has_right, right))
    for side, there, device in sides:
        @pl.when(there)
        def _():
            copy_q_flank(side, device).wait_recv()

    stats = [jnp.zeros((GROUP, DIM), F32)] * 2
    for head in range(HEADS):
        at = lanes(head)
        for side in range(2):
            part = pl.ds(side * (TOKENS - FLANK), FLANK)
            k = jnp.concatenate([kv_all[f, part, at] for f in (0, 1, 2, 0)], axis=0)
            v = jnp.concatenate([kv_all[FRAMES + f, part, at] for f in (0, 1, 2, 0)], axis=0)
            o, stats[side] = guest(head, stats[side], q_flank[side, :, at], k, v, bias_flank[side])
            send_o[2 + side, :, at] = o
    for side, there, device in sides:
        send_s[2 + side] = stats[side]

        @pl.when(there)
        def _():
            copy_flank_o(side, device).start()
            copy_flank_s(side, device).start()

    def near_head(side, head, stat):
        at = lanes(head)
        part = pl.ds(pl.multiple_of(side * EDGE, EDGE), EDGE)
        k = jnp.concatenate([kv_pack[f, part, at] for f in (0, 1, 2, 0)], axis=0)
        v = jnp.concatenate([kv_pack[FRAMES + f, part, at] for f in (0, 1, 2, 0)], axis=0)
        o, stat = guest(head, stat, q_edge[side, :, at], k, v, bias_near[side])
        send_o[side, :, at] = o
        return stat

    def far_head(side, head, stat):
        at = lanes(head)
        part = pl.ds(pl.multiple_of(side * EDGE, EDGE), EDGE)

        def keys(kv):
            pieces = []
            for f in range(FRAMES):
                pieces.append(kv_pack[kv * FRAMES + f, part, at])
                pieces.append(ext[kv * FRAMES + f, :, at])
            return jnp.concatenate(pieces, axis=0)

        o, stat = guest(head, stat, q_edge[side, :, at], keys(0), keys(1), bias_far[...])
        send_o[side, :, at] = o
        return stat

    def edge_of(turn):
        side = (turn + flip) % 2
        there = jnp.where(side == 0, has_up.astype(jnp.int32), has_down.astype(jnp.int32)) > 0
        return side, there, (h - 1 + 2 * side, w)

    per = HEADS // CHUNKS
    side, there, device = edge_of(0)

    @pl.when(there)
    def _():
        for c in range(CHUNKS):
            copy_q_edge(side, c, device).wait_recv()
        stat = jnp.zeros((GROUP, DIM), F32)
        for head in range(HEADS):
            stat = near_head(side, head, stat)
        send_s[side] = stat
        for c in range(CHUNKS):
            copy_edge_o(side, c, device).start()
        copy_edge_s(side, device).start()

    for t, (there, device) in enumerate(corners):
        @pl.when(there)
        def _():
            copy_q_corner(CORNERS - 1 - t, device).wait_recv()

    stat = jnp.zeros((GROUP, DIM), F32)
    for head in range(HEADS):
        at = lanes(head)

        def corner_keys(kv):
            pieces = []
            for f in (0, 1, 2, 0):
                for t in range(CORNERS):
                    pieces.append(kv_pack[kv * FRAMES + f, corner_rows(t), at])
            return jnp.concatenate(pieces, axis=0)

        o, stat = guest(
            head, stat, q_corner[:, at], corner_keys(0), corner_keys(1), bias_corner[...]
        )
        send_o[4, :, at] = o
    send_s[4] = stat
    for t, (there, device) in enumerate(corners):
        @pl.when(there)
        def _():
            copy_corner_o(t, device).start()
            copy_corner_s(t, device).start()

    for side, there, device in sides:
        @pl.when(there & far)
        def _():
            copy_ext(side, device).wait_recv()

    side1, there1, device1 = edge_of(1)

    @pl.when(there1)
    def _():
        stat = jnp.zeros((GROUP, DIM), F32)
        for c in range(CHUNKS):
            copy_q_edge(side1, c, device1).wait_recv()
            for i in range(per):
                stat = far_head(side1, c * per + i, stat)

            @pl.when(far_via)
            def _():
                to_via_o(c).start()

            @pl.when(jnp.logical_not(far_via))
            def _():
                copy_edge_o(side1, c, device1).start()

        send_s[side1] = stat

        @pl.when(far_via)
        def _():
            to_via_s().start()

        @pl.when(jnp.logical_not(far_via))
        def _():
            copy_edge_s(side1, device1).start()

    @pl.when(serves)
    def _():
        for c in range(CHUNKS):
            to_via_q(c).wait_recv()
            onward_q(c).start()

    for side, there, device in sides:
        @pl.when(there)
        def _():
            copy_flank_o(1 - side, device).wait_recv()
            copy_flank_s(1 - side, device).wait_recv()

    def column(stat, index):
        return jnp.concatenate(
            [stat[:, 32 * t + index : 32 * t + index + 1] for t in range(4)], axis=0
        )

    def merge(own, other):
        (m0, l0, o0), (m1, l1, o1) = own, other
        top = jnp.maximum(m0, m1)
        a0, a1 = jnp.exp2(m0 - top), jnp.exp2(m1 - top)
        return top, a0 * l0 + a1 * jnp.maximum(l1, 0.0), a0 * o0 + a1 * o1.astype(F32)

    wide_lane = iota((TOKENS, DIM), 1)
    own_stat = jnp.zeros((TOKENS, DIM), F32)
    for head in range(HEADS):
        at = lanes(head)
        for side in range(2):
            part = pl.ds(side * (TOKENS - FLANK), FLANK)
            stat = flank_s[side]
            top, total, mixed = merge(
                (own_m[head, part], own_l[head, part], own_o[head, part]),
                (column(stat, head), column(stat, HEADS + head), flank_o[side, :, at]),
            )
            own_m[head, part] = top
            own_l[head, part] = total
            own_o[head, part] = mixed
        total = own_l[head]
        high = total.astype(BF16).astype(F32)
        own_stat = jnp.where(wide_lane == head, own_m[head], own_stat)
        own_stat = jnp.where(wide_lane == HEADS + head, high, own_stat)
        own_stat = jnp.where(wide_lane == 2 * HEADS + head, total - high, own_stat)
    packed_stat = dot_nn(pick[...], own_stat.astype(BF16))
    inner = iota((TOKENS, DIM), 0) % ROWS
    inner = (inner >= RADIUS) & (inner < ROWS - RADIUS)
    for head in range(HEADS):
        at = lanes(head)
        o = own_o[head]
        high = o.astype(BF16)
        rest = (o - high.astype(F32)).astype(BF16)
        edge_own_o[head] = dot_nn(pick[...], high) + dot_nn(pick[...], rest)
        edge_own_m[head] = jnp.broadcast_to(packed_stat[:, head : head + 1], (2 * EDGE, DIM))
        edge_own_l[head] = jnp.broadcast_to(
            packed_stat[:, HEADS + head : HEADS + head + 1]
            + packed_stat[:, 2 * HEADS + head : 2 * HEADS + head + 1],
            (2 * EDGE, DIM),
        )
        out[:, at] = jnp.where(inner, o / own_l[head], 0.0).astype(BF16)

    for t, (there, device) in enumerate(corners):
        @pl.when(there)
        def _():
            copy_corner_o(CORNERS - 1 - t, device).wait_recv()
            copy_corner_s(CORNERS - 1 - t, device).wait_recv()

    slot = iota((EDGE, DIM), 0) // RADIUS
    real = real_slot(slot)
    for side in range(2):
        for lr in range(2):
            t = 2 * side + lr
            part = pl.ds(side * EDGE + lr * (EDGE - CORNER), CORNER)
            first = 32 * (CORNERS - 1 - t)
            stat = corner_s[t]
            for head in range(HEADS):
                m1 = stat[:, first + head : first + head + 1]
                l1 = stat[:, first + HEADS + head : first + HEADS + head + 1]
                o1 = corner_o[t * CORNER : (t + 1) * CORNER, lanes(head)]
                top, total, mixed = merge(
                    (edge_own_m[head, part], edge_own_l[head, part], edge_own_o[head, part]),
                    (m1, l1, o1),
                )
                edge_own_m[head, part] = top
                edge_own_l[head, part] = total
                edge_own_o[head, part] = mixed

    for turn in range(2):
        side, there, device = edge_of(turn)
        part = pl.ds(pl.multiple_of(side * EDGE, EDGE), EDGE)
        place = jnp.where(side == 0, spread[:, 0:EDGE], spread[:, EDGE : 2 * EDGE])

        @pl.when(there)
        def _():
            for c in range(CHUNKS):
                copy_edge_o(1 - side, c, device).wait_recv()
            copy_edge_s(1 - side, device).wait_recv()

        stat = edge_s[side]
        for head in range(HEADS):
            at = lanes(head)
            top, total, mixed = merge(
                (edge_own_m[head, part], edge_own_l[head, part], edge_own_o[head, part]),
                (column(stat, head), column(stat, HEADS + head), edge_o[side, :, at]),
            )
            done = jnp.where(real, mixed / total, 0.0).astype(BF16)
            out[:, at] = out[:, at] + dot_nn(place, done).astype(BF16)

    @pl.when(serves)
    def _():
        for c in range(CHUNKS):
            to_via_o(c).wait_recv()
            onward_o(c).start()
        to_via_s().wait_recv()
        onward_s().start()
        for c in range(CHUNKS):
            onward_q(c).wait_send()
            onward_o(c).wait_send()
        onward_s().wait_send()

    @pl.when(far_via)
    def _():
        for c in range(CHUNKS):
            to_via_q(c).wait_send()
            to_via_o(c).wait_send()
        to_via_s().wait_send()

    @pl.when(far_direct)
    def _():
        for c in range(CHUNKS):
            far_q(c).wait_send()
            copy_edge_o(side1, c, device1).wait_send()
        copy_edge_s(side1, device1).wait_send()

    for c in range(CHUNKS):
        @pl.when(near_down)
        def _():
            copy_q_edge(0, c, down).wait_send()
            copy_edge_o(1, c, down).wait_send()

        @pl.when(near_up)
        def _():
            copy_q_edge(1, c, up).wait_send()
            copy_edge_o(0, c, up).wait_send()

    @pl.when(near_down)
    def _():
        copy_edge_s(1, down).wait_send()

    @pl.when(near_up)
    def _():
        copy_edge_s(0, up).wait_send()

    for side, there, device in ((0, has_right, right), (1, has_left, left)):
        @pl.when(there)
        def _():
            copy_q_flank(side, device).wait_send()
            copy_flank_o(1 - side, device).wait_send()
            copy_flank_s(1 - side, device).wait_send()

        @pl.when(there & far)
        def _():
            copy_ext(side, device).wait_send()

    for t, (there, device) in enumerate(corners):
        @pl.when(there)
        def _():
            copy_q_corner(t, device).wait_send()
            copy_corner_o(t, device).wait_send()
            copy_corner_s(t, device).wait_send()


def on_device(nh, nw, queries, kv_new, kv_past):
    wide = HEADS * DIM
    hbm = pl.BlockSpec(memory_space=pltpu.HBM)
    dma = pltpu.SemaphoreType.DMA
    queries = queries.transpose(1, 0, 2).reshape(TOKENS, wide)
    kv_new = kv_new.transpose(0, 2, 1, 3).reshape(2, TOKENS, wide)
    kv_past = kv_past.transpose(0, 1, 3, 2, 4).reshape(FRAMES - 1, 2, TOKENS, wide)
    out = pl.pallas_call(
        functools.partial(kernel, nh, nw),
        out_shape=jax.ShapeDtypeStruct((TOKENS, wide), BF16),
        in_specs=[hbm] * 3,
        out_specs=pl.BlockSpec(memory_space=pltpu.VMEM),
        scratch_shapes=[
            pltpu.VMEM((TOKENS, wide), BF16),
            pltpu.VMEM((2 * FRAMES, TOKENS, wide), BF16),
            pltpu.VMEM((2 * EDGE, wide), BF16),
            pltpu.VMEM((2 * FRAMES, 2 * EDGE, wide), BF16),
            pltpu.VMEM((2, EDGE, wide), BF16),
            pltpu.VMEM((2, FLANK, wide), BF16),
            pltpu.VMEM((CORNERS * CORNER, wide), BF16),
            pltpu.VMEM((2 * FRAMES, 2 * CORNER, wide), BF16),
            pltpu.VMEM((HEADS, TOKENS, DIM), F32),
            pltpu.VMEM((HEADS, TOKENS, DIM), F32),
            pltpu.VMEM((HEADS, TOKENS, DIM), F32),
            pltpu.VMEM((HEADS, 2 * EDGE, DIM), F32),
            pltpu.VMEM((HEADS, 2 * EDGE, DIM), F32),
            pltpu.VMEM((HEADS, 2 * EDGE, DIM), F32),
            pltpu.VMEM((5, EDGE, wide), BF16),
            pltpu.VMEM((5, GROUP, DIM), F32),
            pltpu.VMEM((2, EDGE, wide), BF16),
            pltpu.VMEM((2, GROUP, DIM), F32),
            pltpu.VMEM((2, FLANK, wide), BF16),
            pltpu.VMEM((2, GROUP, DIM), F32),
            pltpu.VMEM((CORNERS * CORNER, wide), BF16),
            pltpu.VMEM((CORNERS, GROUP, DIM), F32),
            pltpu.VMEM((EDGE, wide), BF16),
            pltpu.VMEM((EDGE, wide), BF16),
            pltpu.VMEM((GROUP, DIM), F32),
            pltpu.VMEM((REACH0, CUT), F32),
            pltpu.VMEM((TOKENS - REACH1, CUT), F32),
            pltpu.VMEM((2, FLANK, (FRAMES + 1) * FLANK), F32),
            pltpu.VMEM((2, EDGE, (FRAMES + 1) * EDGE), F32),
            pltpu.VMEM((EDGE, FRAMES * SPAN), F32),
            pltpu.VMEM((EDGE, (FRAMES + 1) * EDGE), F32),
            pltpu.VMEM((2 * EDGE, TOKENS), BF16),
            pltpu.VMEM((TOKENS, 2 * EDGE), BF16),
            dma((1 + 2 * FRAMES,)),
            dma((2, 2, CHUNKS)),
            dma((2, 2)),
            dma((2, CORNERS)),
            dma((2, 2)),
            dma((2, 2, CHUNKS)),
            dma((2, 2)),
            dma((2, CORNERS)),
            dma((2, 8)),
            dma((2, 2 * CHUNKS + 1)),
            dma((2 * CHUNKS + 1,)),
        ],
        compiler_params=pltpu.CompilerParams(
            collective_id=0, has_side_effects=True, vmem_limit_bytes=VMEM_BYTES
        ),
    )(queries, kv_new, kv_past)
    return out.reshape(COLS, ROWS, wide).transpose(1, 0, 2)


def solution(mesh):
    return jax.shard_map(
        functools.partial(on_device, mesh.shape["ha"], mesh.shape["wa"]),
        mesh=mesh,
        in_specs=(P("ha", "wa", None), P(None, "ha", "wa", None), P(None, None, "ha", "wa", None)),
        out_specs=P("ha", "wa", None),
        check_vma=False,
    )
```
